512 devices in a mesh: expert: 128 (over y, z, x_lo), dp: 4 (over x_hi, core).
Axes of the slice: x: 4 (x_hi: 2, x_lo: 2; x = x_hi * 2 + x_lo), y: 4, z: 16, core: 2. Of those that a mesh axis runs over, the one named last changes fastest.
Arguments:
- tokens: bfloat16 [65536, 1024], P(('expert', 'dp')), may hold values from -6 to 6
- cotangent: bfloat16 [65536, 1024], P(('expert', 'dp')), may hold values from -6 to 6
- route_ids: int32 [65536, 2], P(('expert', 'dp')), may hold values from 0 to 127, all different within a row; in each aligned block of 128 rows (0 to 127, 128 to 255, ...) at most 3 rows name the same one
- gate_prob: bfloat16 [65536, 2], P(('expert', 'dp')), may hold values from 0.099609375 to 0.59765625
- swap_partner: int32 [128], replicated, may hold values from 0 to 127, as said below
- expert_weights: bfloat16 [128, 3, 1024, 384], P('expert', None, 'dp'), may hold values from -0.1875 to 0.1875
- first_moment: float32 [128, 3, 1024, 384], P('expert', None, 'dp'), may hold values from -6 to 6
- second_moment: float32 [128, 3, 1024, 384], P('expert', None, 'dp'), may hold values from 1 to 30
Outputs:
- token_grad: bfloat16 [65536, 1024], P(('expert', 'dp'))
- gate_grad: bfloat16 [65536, 2], P(('expert', 'dp'))
- adam_update: bfloat16 [128, 3, 1024, 384], P('expert', None, 'dp')
The draws below stay inside these ranges and needn't reach their ends.
Inputs may be any that keep to these rules, and one draw needn't show every extreme that they name: `route_ids`: each row names 2 different experts; among the 128 tokens of one device no expert is named more than 3 times, a bound that some block reaches. `swap_partner`: s[s[e]] = e for every e; exactly 32 pairs of experts trade slots, every other expert keeps its own.
All inputs are finite; a program needn't handle non-finite values.
Results may differ from the reference program's by a relative error of at most 0.013.
Values may be sent and summed in bfloat16 or wider, within the bound.
No kernel may reach another device: no remote copies, remote signals or barrier semaphores. Data moves between devices by JAX's collectives and lax.ppermute only.
A program may use at most 64 MiB of HBM per device.

```python
import math
import jax
import jax.numpy as jnp
import numpy as np
from jax import lax

D = 1024
FW = 384
TOPK = 2
STEP = 100
TOK_DEV = 128
EXPERTS = 128
TOKENS = 65536
CAP = 3
N_EXPERT = 128
N_DP = 4


def draw_swap_partner(key, part):
    shuffled = jax.random.permutation(key, EXPERTS).astype(jnp.int32)
    pair_count = EXPERTS // 4
    first_half = shuffled[0:2 * pair_count:2]
    second_half = shuffled[1:2 * pair_count:2]
    partner = jnp.arange(EXPERTS, dtype=jnp.int32)
    partner = partner.at[first_half].set(second_half)
    partner = partner.at[second_half].set(first_half)
    return partner.astype(jnp.int32)


def shard_levels(key, dims, split, low, largest):
    def one(axis_at, parts):
        draws = jax.random.uniform(jax.random.fold_in(jax.random.fold_in(key, 6), axis_at), (parts,), jnp.float32, low / len(split), largest / len(split))
        return jnp.repeat(jnp.exp(draws), dims[axis_at] // parts).reshape((-1,) + (1,) * (len(dims) - axis_at - 1))

    loudness = one(*split[0])
    for cut in split[1:]:
        loudness = loudness * one(*cut)
    return loudness


def shared_out(stream_key, own, number, rows, amount, top, most, lean):
    sequence = jax.random.permutation(stream_key, amount)
    heavy_load, common = load_shares(amount, rows * top, most, lean, True), load_shares(amount, rows * top, most, lean, False)
    places = jnp.arange(amount)

    def named(sizes, turn):
        used = int((sizes > 0).sum())
        fixed = max(1, used // 4)
        passed = fixed + (places - fixed + turn * (used - fixed)) % max(1, amount - fixed)
        return jnp.zeros((amount,), jnp.int32).at[sequence[jnp.where(places < fixed, places, passed)]].set(jnp.asarray(sizes, jnp.int32))

    sizes = jnp.where(number % 4 == 0, named(heavy_load, number // 4), named(common, number - number // 4 - 1))
    mixed = jax.random.permutation(jax.random.fold_in(own, 3), amount)
    source_of, taker = mixed[0:amount // 2 * 2:2], mixed[1:amount // 2 * 2:2]
    margin = jnp.minimum(sizes[source_of] - 1, most - sizes[taker]) // 2
    margin = jnp.where((source_of == sequence[0]) | (taker == sequence[0]) | (sizes[taker] == 0), 0, jnp.maximum(margin, 0))
    passed = jax.random.randint(jax.random.fold_in(own, 4), (amount // 2,), 0, 1 << 20) % (margin + 1)
    sizes = sizes.at[source_of].add(-passed).at[taker].add(passed)
    items = jnp.searchsorted(jnp.cumsum(sizes), jnp.arange(rows * top), side="right").astype(jnp.int32)
    table = items.reshape(top, rows).T
    table = table[jax.random.permutation(jax.random.fold_in(own, 1), rows)]
    turn = jax.random.randint(jax.random.fold_in(own, 2), (rows, 1), 0, top)
    return jnp.take_along_axis(table, (jnp.arange(top)[None, :] + turn) % top, axis=1)


def load_shares(amount, total, limit, lean, full):
    portions = [(1 << 20) // math.isqrt(standing ** lean) + 1 for standing in range(1, amount + 1)]
    largest = limit if full else min(limit, max(-(-total // amount), total * portions[0] // sum(portions)))
    least = 1 if total - largest >= amount - 1 else 0
    given, rest = [largest] + [least] * (amount - 1), total - largest - least * (amount - 1)
    while rest > 0:
        movable = [i for i in range(1, amount) if given[i] < largest] or [i for i in range(1, amount) if given[i] < limit]
        pool, remaining = sum([portions[i] for i in movable]), rest
        for i in movable:
            extra = min(limit - given[i], max(1, remaining * portions[i] // pool), rest)
            given[i] = given[i] + extra
            rest = rest - extra
    return np.array(given)


def noise(key, shape, scale, most, shards=(), kind=jnp.bfloat16):
    result = jax.random.normal(key, shape, jnp.float32) * scale
    if len(shards) > 0:
        result = shard_levels(key, shape, shards, -0.22, 0.18) * result
    return jnp.clip(result, min=-most, max=most).astype(kind)


def setup_inputs(seed: int = 0) -> dict:
    seeds = jax.random.split(jax.random.key(seed), 9)
    tokens = noise(seeds[0], (TOKENS, D), 1.0, 6.0, ((0, 512),))
    cotangent = noise(seeds[1], (TOKENS, D), 1.0, 6.0, ((0, 512),))
    route_ids_keys = jax.random.split(jax.random.fold_in(seeds[2], 1), TOKENS // TOK_DEV)
    route_ids_turns = jax.random.permutation(jax.random.fold_in(seeds[2], 3), TOKENS // TOK_DEV)
    route_ids = jax.vmap(lambda own, number: shared_out(jax.random.fold_in(seeds[2], 2), own, number, TOK_DEV, EXPERTS, TOPK, CAP, 2))(route_ids_keys, route_ids_turns).reshape((TOKENS, TOPK))
    gate_prob = jnp.clip(0.099609375 + 0.49804688 * jax.random.uniform(seeds[3], (TOKENS, TOPK), jnp.float32) ** shard_levels(seeds[3], (TOKENS, TOPK), ((0, 512),), -0.2, 0.2), 0.099609375, 0.59765625).astype(jnp.bfloat16)
    swap_partner = draw_swap_partner(jax.random.fold_in(seeds[8], 71), 0)
    expert_weights = noise(seeds[5], (EXPERTS, 3, D, FW), D ** -0.5, 0.1875, ((0, 128), (2, 4)))
    first_moment = noise(seeds[6], (EXPERTS, 3, D, FW), 1.0, 6.0, ((0, 128), (2, 4)), jnp.float32)
    second_moment = jnp.clip(jnp.exp(math.log(30.0) - 3.4011974 * jax.random.uniform(seeds[7], (EXPERTS, 3, D, FW), jnp.float32) ** shard_levels(seeds[7], (EXPERTS, 3, D, FW), ((0, 128), (2, 4)), -0.2, 0.2)), 1.0, 30.0)
    return {"tokens": tokens, "cotangent": cotangent, "route_ids": route_ids, "gate_prob": gate_prob, "swap_partner": swap_partner, "expert_weights": expert_weights, "first_moment": first_moment, "second_moment": second_moment}


BETA_ONE = 0.9
BETA_TWO = 0.95
ADAM_EPS = 1e-08

def round_half(value):
    return lax.optimization_barrier(value.astype(jnp.bfloat16)).astype(jnp.float32)

def silu_parts(pre_act):
    sigmoid_val = jax.nn.sigmoid(pre_act)
    return (pre_act * sigmoid_val, sigmoid_val * (1.0 + pre_act * (1.0 - sigmoid_val)))

def reference(tokens, cotangent, route_ids, gate_prob, swap_partner, expert_weights, first_moment, second_moment):
    total_rows = TOKENS * TOPK
    block_rows = TOK_DEV * TOPK
    blocks = TOKENS // TOK_DEV
    flat_ids = route_ids.reshape(-1).astype(jnp.int32)
    one_hot = (flat_ids.reshape(blocks, block_rows)[:, :, None] == jnp.arange(EXPERTS, dtype=jnp.int32)[None, None, :]).astype(jnp.int32)
    running = jnp.cumsum(one_hot, axis=1) - 1
    slot_rank = lax.optimization_barrier(jnp.sum(running * one_hot, axis=2)).reshape(-1).astype(jnp.int32)
    block_index = (jnp.arange(total_rows, dtype=jnp.int32) // block_rows).astype(jnp.int32)
    row_table = jnp.full((EXPERTS, blocks, CAP), total_rows, jnp.int32)
    row_table = row_table.at[flat_ids, block_index, slot_rank].set(jnp.arange(total_rows, dtype=jnp.int32))
    row_table = row_table.reshape(EXPERTS, N_EXPERT, N_DP, CAP).transpose(0, 2, 1, 3).reshape(EXPERTS, N_DP, N_EXPERT * CAP)
    padded_tokens = jnp.concatenate([tokens, jnp.zeros((1, D), tokens.dtype)], axis=0)
    padded_cot = jnp.concatenate([cotangent, jnp.zeros((1, D), cotangent.dtype)], axis=0)
    padded_prob = jnp.concatenate([gate_prob.reshape(-1), jnp.zeros((1,), gate_prob.dtype)], axis=0)
    bias_one = 1.0 - BETA_ONE ** STEP
    bias_two = 1.0 - BETA_TWO ** STEP

    def one_expert(totals, inputs):
        grad_acc, gate_acc = totals
        row_ids, weights, moment_one, moment_two = inputs
        token_index = jnp.where(row_ids < total_rows, row_ids // TOPK, TOKENS).astype(jnp.int32)
        rows_in = padded_tokens[token_index].astype(jnp.float32)
        rows_cot = padded_cot[token_index].astype(jnp.float32)
        rows_prob = padded_prob[row_ids].astype(jnp.float32)
        w_gate = weights[0].astype(jnp.float32)
        w_up = weights[1].astype(jnp.float32)
        w_down = weights[2].astype(jnp.float32)
        pre_gate = jnp.einsum('jrd,df->jrf', rows_in, w_gate)
        pre_up = jnp.einsum('jrd,df->jrf', rows_in, w_up)
        silu_gate, silu_slope = silu_parts(pre_gate)
        hidden = round_half(silu_gate * pre_up)
        output = jnp.einsum('jrf,df->jrd', hidden, w_down)
        gate_term = round_half(lax.optimization_barrier(jnp.sum(output * rows_cot, axis=2)))
        scaled = round_half(rows_prob[:, :, None] * rows_cot)
        d_hidden = jnp.einsum('jrd,df->jrf', scaled, w_down)
        d_gate = round_half(d_hidden * pre_up * silu_slope)
        d_up = round_half(d_hidden * silu_gate)
        d_rows = round_half(jnp.einsum('jrf,df->jrd', d_gate, w_gate) + jnp.einsum('jrf,df->jrd', d_up, w_up))
        partial_value = jnp.stack([jnp.einsum('jrd,jrf->jdf', rows_in, d_gate), jnp.einsum('jrd,jrf->jdf', rows_in, d_up), jnp.einsum('jrd,jrf->jdf', scaled, hidden)], axis=1)
        gradient = lax.optimization_barrier(jnp.sum(round_half(partial_value), axis=0))
        first_new = BETA_ONE * moment_one + (1.0 - BETA_ONE) * gradient
        second_new = BETA_TWO * moment_two + (1.0 - BETA_TWO) * gradient * gradient
        update = (first_new / bias_one / (jnp.sqrt(second_new / bias_two) + ADAM_EPS)).astype(jnp.bfloat16)
        grad_acc = grad_acc.at[token_index.reshape(-1)].add(d_rows.reshape(-1, D))
        gate_acc = gate_acc.at[row_ids.reshape(-1)].add(gate_term.reshape(-1))
        return ((grad_acc, gate_acc), update)
    start = (jnp.zeros((TOKENS + 1, D), jnp.float32), jnp.zeros((total_rows + 1,), jnp.float32))
    (grad_acc, gate_acc), updates = lax.scan(one_expert, start, (row_table, expert_weights, first_moment, second_moment))
    token_grad = grad_acc[:TOKENS].astype(jnp.bfloat16)
    gate_grad = gate_acc[:total_rows].reshape(TOKENS, TOPK).astype(jnp.bfloat16)
    adam_update = updates[swap_partner]
    return (token_grad, gate_grad, adam_update)
```

```python
import jax
import jax.numpy as jnp
from jax import lax
from jax.sharding import PartitionSpec as P

STEP = 100
BETA_ONE = 0.9
BETA_TWO = 0.95
ADAM_EPS = 1e-08
CAP = 3


def silu_parts(pre_act):
    sigmoid_val = jax.nn.sigmoid(pre_act)
    return (pre_act * sigmoid_val, sigmoid_val * (1.0 + pre_act * (1.0 - sigmoid_val)))


def adam_step(gradient, moment_one, moment_two):
    first_new = BETA_ONE * moment_one + (1.0 - BETA_ONE) * gradient
    second_new = BETA_TWO * moment_two + (1.0 - BETA_TWO) * gradient * gradient
    first_hat = first_new / (1.0 - BETA_ONE**STEP)
    second_hat = second_new / (1.0 - BETA_TWO**STEP)
    return (first_hat / (jnp.sqrt(second_hat) + ADAM_EPS)).astype(jnp.bfloat16)


def exchange(x):
    return lax.all_to_all(x, "expert", split_axis=0, concat_axis=0, tiled=True)


def on_device(
    tokens,
    cotangent,
    route_ids,
    gate_prob,
    swap_partner,
    expert_weights,
    first_moment,
    second_moment,
):
    groups = lax.axis_size("expert")
    tok_count, width = tokens.shape
    rows = groups * CAP
    f32, bf16 = jnp.float32, jnp.bfloat16

    whole = lax.all_gather(expert_weights, "dp", axis=2, tiled=True)[0]

    hot = (route_ids[:, :, None] == jnp.arange(groups, dtype=jnp.int32)).astype(bf16)
    named = hot[:, 0] + hot[:, 1]
    prob_at = hot[:, 0] * gate_prob[:, :1] + hot[:, 1] * gate_prob[:, 1:]
    step = jnp.arange(tok_count, dtype=jnp.int32)
    earlier = (step[None, :] < step[:, None]).astype(bf16)
    rank = jnp.dot(earlier, named, preferred_element_type=f32)
    picks = jnp.stack([jnp.where(rank == r, named, 0) for r in range(CAP)])
    picks_prob = picks * prob_at
    sent_x = jnp.einsum("rte,td->erd", picks, tokens, preferred_element_type=f32)
    sent_q = jnp.einsum("rte,td->erd", picks_prob, cotangent, preferred_element_type=f32)
    sent = jnp.concatenate([sent_x.astype(bf16), sent_q.astype(bf16)], axis=1)
    got = exchange(sent.reshape(groups, 6, 8, 128)).reshape(groups, 6, width)
    rows_in = got[:, :CAP].reshape(rows, width)
    scaled = got[:, CAP:].reshape(rows, width)

    pre_gate = jnp.dot(rows_in, whole[0], preferred_element_type=f32)
    pre_up = jnp.dot(rows_in, whole[1], preferred_element_type=f32)
    d_hidden = jnp.dot(scaled, whole[2], preferred_element_type=f32)
    silu_gate, silu_slope = silu_parts(pre_gate)
    hidden = (silu_gate * pre_up).astype(bf16)
    d_gate = (d_hidden * pre_up * silu_slope).astype(bf16)
    d_up = (d_hidden * silu_gate).astype(bf16)
    over_rows = (((0,), (0,)), ((), ()))
    partial = jnp.stack(
        [
            lax.dot_general(rows_in, d_gate, over_rows, preferred_element_type=f32),
            lax.dot_general(rows_in, d_up, over_rows, preferred_element_type=f32),
            lax.dot_general(scaled, hidden, over_rows, preferred_element_type=f32),
        ]
    ).astype(bf16)
    gradient = lax.psum_scatter(partial, "dp", scatter_dimension=1, tiled=True).astype(f32)

    gate_term = jnp.sum(hidden.astype(f32) * d_hidden, axis=1).astype(bf16)
    transposed = (((1,), (1,)), ((), ()))
    d_rows = (
        lax.dot_general(d_gate, whole[0], transposed, preferred_element_type=f32)
        + lax.dot_general(d_up, whole[1], transposed, preferred_element_type=f32)
    ).astype(bf16)
    returned = jnp.concatenate(
        [
            d_rows.reshape(groups, CAP * width),
            jnp.pad(gate_term.reshape(groups, CAP), ((0, 0), (0, 128 - CAP))),
        ],
        axis=1,
    )
    back = exchange(returned)
    back_rows = back[:, : CAP * width].reshape(groups, CAP, width)
    token_grad = jnp.einsum("rte,erd->td", picks, back_rows, preferred_element_type=f32).astype(bf16)
    back_gate = back[:, CAP * width : CAP * width + CAP].astype(f32)
    gate_at = jnp.sum(picks.astype(f32) * back_gate.T[:, None, :], axis=0)
    gate_grad = jnp.sum(hot.astype(f32) * gate_at[:, None, :], axis=2) / gate_prob.astype(f32)

    update = adam_step(gradient, first_moment[0], second_moment[0])
    spread = exchange(update.reshape(groups, -1))
    routed = exchange(jnp.take(spread, swap_partner, axis=0))
    return (token_grad, gate_grad.astype(bf16), routed.reshape(expert_weights.shape))


def solution(mesh):
    placed = (
        P(("expert", "dp"), None),
        P(("expert", "dp"), None),
        P(("expert", "dp"), None),
        P(("expert", "dp"), None),
        P(),
        P("expert", None, "dp", None),
        P("expert", None, "dp", None),
        P("expert", None, "dp", None),
    )
    return jax.shard_map(
        on_device,
        mesh=mesh,
        in_specs=placed,
        out_specs=(
            P(("expert", "dp"), None),
            P(("expert", "dp"), None),
            P("expert", None, "dp", None),
        ),
        check_vma=False,
    )
```

```python
import jax
import jax.numpy as jnp
from jax import lax
from jax.sharding import PartitionSpec as P

STEP = 100
BETA_ONE = 0.9
BETA_TWO = 0.95
ADAM_EPS = 1e-08
CAP = 3


def silu_parts(pre_act):
    sigmoid_val = jax.nn.sigmoid(pre_act)
    return (pre_act * sigmoid_val, sigmoid_val * (1.0 + pre_act * (1.0 - sigmoid_val)))


def adam_step(gradient, moment_one, moment_two):
    first_new = BETA_ONE * moment_one + (1.0 - BETA_ONE) * gradient
    second_new = BETA_TWO * moment_two + (1.0 - BETA_TWO) * gradient * gradient
    first_hat = first_new / (1.0 - BETA_ONE**STEP)
    second_hat = second_new / (1.0 - BETA_TWO**STEP)
    return (first_hat / (jnp.sqrt(second_hat) + ADAM_EPS)).astype(jnp.bfloat16)


def exchange(x):
    return lax.all_to_all(x, "expert", split_axis=0, concat_axis=0, tiled=True)


def on_device(
    tokens,
    cotangent,
    route_ids,
    gate_prob,
    swap_partner,
    expert_weights,
    first_moment,
    second_moment,
):
    groups = lax.axis_size("expert")
    tok_count, width = tokens.shape
    rows = groups * CAP
    f32, bf16 = jnp.float32, jnp.bfloat16

    whole = lax.all_gather(expert_weights, "dp", axis=2, tiled=True)[0]

    hot = (route_ids[:, :, None] == jnp.arange(groups, dtype=jnp.int32)).astype(bf16)
    named = hot[:, 0] + hot[:, 1]
    prob_at = hot[:, 0] * gate_prob[:, :1] + hot[:, 1] * gate_prob[:, 1:]
    step = jnp.arange(tok_count, dtype=jnp.int32)
    earlier = (step[None, :] < step[:, None]).astype(bf16)
    rank = jnp.dot(earlier, named, preferred_element_type=f32)
    picks = jnp.stack([jnp.where(rank == r, named, 0) for r in range(CAP)])
    picks_prob = picks * prob_at
    sent_x = jnp.einsum("rte,td->erd", picks, tokens, preferred_element_type=f32)
    sent_q = jnp.einsum("rte,td->erd", picks_prob, cotangent, preferred_element_type=f32)
    sent = jnp.concatenate([sent_x.astype(bf16), sent_q.astype(bf16)], axis=1)
    got = exchange(sent.reshape(groups, 6, 8, 128)).reshape(groups, 6, width)
    rows_in = got[:, :CAP].reshape(rows, width)
    scaled = got[:, CAP:].reshape(rows, width)

    pre_gate = jnp.dot(rows_in, whole[0], preferred_element_type=f32)
    pre_up = jnp.dot(rows_in, whole[1], preferred_element_type=f32)
    d_hidden = jnp.dot(scaled, whole[2], preferred_element_type=f32)
    silu_gate, silu_slope = silu_parts(pre_gate)
    hidden = (silu_gate * pre_up).astype(bf16)
    d_gate = (d_hidden * pre_up * silu_slope).astype(bf16)
    d_up = (d_hidden * silu_gate).astype(bf16)
    gate_term = jnp.sum(hidden.astype(f32) * d_hidden, axis=1).astype(bf16)
    transposed = (((1,), (1,)), ((), ()))
    d_rows = (
        lax.dot_general(d_gate, whole[0], transposed, preferred_element_type=f32)
        + lax.dot_general(d_up, whole[1], transposed, preferred_element_type=f32)
    ).astype(bf16)
    returned = jnp.concatenate(
        [
            d_rows.reshape(groups, CAP * width),
            jnp.pad(gate_term.reshape(groups, CAP), ((0, 0), (0, 128 - CAP))),
        ],
        axis=1,
    )
    rows_in, scaled, d_gate, d_up, hidden, returned = lax.optimization_barrier(
        (rows_in, scaled, d_gate, d_up, hidden, returned)
    )
    back = exchange(returned)
    over_rows = (((0,), (0,)), ((), ()))
    partial = jnp.stack(
        [
            lax.dot_general(rows_in, d_gate, over_rows, preferred_element_type=f32),
            lax.dot_general(rows_in, d_up, over_rows, preferred_element_type=f32),
            lax.dot_general(scaled, hidden, over_rows, preferred_element_type=f32),
        ]
    ).astype(bf16)
    gradient = lax.psum_scatter(partial, "dp", scatter_dimension=1, tiled=True).astype(f32)

    back, gradient = lax.optimization_barrier((back, gradient))

    back_rows = back[:, : CAP * width].reshape(groups, CAP, width)
    token_grad = jnp.einsum("rte,erd->td", picks, back_rows, preferred_element_type=f32).astype(bf16)
    back_gate = back[:, CAP * width : CAP * width + CAP].astype(f32)
    gate_at = jnp.sum(picks.astype(f32) * back_gate.T[:, None, :], axis=0)
    gate_grad = jnp.sum(hot.astype(f32) * gate_at[:, None, :], axis=2) / gate_prob.astype(f32)

    update = adam_step(gradient, first_moment[0], second_moment[0])
    spread = exchange(update.reshape(groups, -1))
    routed = exchange(jnp.take(spread, swap_partner, axis=0))
    return (token_grad, gate_grad.astype(bf16), routed.reshape(expert_weights.shape))


def solution(mesh):
    placed = (
        P(("expert", "dp"), None),
        P(("expert", "dp"), None),
        P(("expert", "dp"), None),
        P(("expert", "dp"), None),
        P(),
        P("expert", None, "dp", None),
        P("expert", None, "dp", None),
        P("expert", None, "dp", None),
    )
    return jax.shard_map(
        on_device,
        mesh=mesh,
        in_specs=placed,
        out_specs=(
            P(("expert", "dp"), None),
            P(("expert", "dp"), None),
            P("expert", None, "dp", None),
        ),
        check_vma=False,
    )
```

```python
import jax
import jax.numpy as jnp
from jax import lax
from jax.experimental import pallas as pl
from jax.experimental.pallas import tpu as pltpu
from jax.sharding import PartitionSpec as P

STEP = 100
BETA_ONE = 0.9
BETA_TWO = 0.95
ADAM_EPS = 1e-08
CAP = 3
LANES = 128
f32, bf16 = jnp.float32, jnp.bfloat16

NN = (((1,), (0,)), ((), ()))
NT = (((1,), (1,)), ((), ()))
TN = (((0,), (0,)), ((), ()))


def mul(a, b, dims):
    return lax.dot_general(a, b, dims, preferred_element_type=f32)


def call(body, outs, scratch, flops, moved):
    return pl.pallas_call(
        body,
        out_shape=outs,
        scratch_shapes=scratch,
        compiler_params=pltpu.CompilerParams(vmem_limit_bytes=48 * 2**20),
        cost_estimate=pl.CostEstimate(flops=flops, bytes_accessed=moved, transcendentals=0),
    )


def exchange(x):
    return lax.all_to_all(x, "expert", split_axis=0, concat_axis=0, tiled=True)


def routing(ids, groups):
    tok_count = ids.shape[1]
    expert = lax.broadcasted_iota(jnp.int32, (groups, tok_count), 0)
    hots = [ids[k : k + 1, :] == expert for k in range(2)]
    named = jnp.where(hots[0] | hots[1], 1.0, 0.0)
    before = lax.broadcasted_iota(jnp.int32, (tok_count, tok_count), 0)
    after = lax.broadcasted_iota(jnp.int32, (tok_count, tok_count), 1)
    earlier = jnp.where(before < after, 1.0, 0.0).astype(bf16)
    rank = mul(named.astype(bf16), earlier, NN)
    return hots, [jnp.where(rank == r, named, 0.0) for r in range(CAP)]


def dispatch_body(ids_ref, prob_ref, tok_ref, cot_ref, out_ref, stage):
    groups, _, sub, _ = out_ref.shape
    chunks = sub // 2
    hots, picks = routing(ids_ref[...], groups)
    prob = prob_ref[...].astype(f32)
    prob_at = jnp.where(hots[0], prob[0:1, :], jnp.where(hots[1], prob[1:2, :], 0.0))
    for r in range(CAP):
        x = mul(picks[r].astype(bf16), tok_ref[...], NN)
        q = mul((picks[r] * prob_at).astype(bf16), cot_ref[...], NN)
        for c in range(chunks):
            cols = slice(c * LANES, (c + 1) * LANES)
            stage[pl.ds(c, groups, stride=sub), :] = x[:, cols]
            stage[pl.ds(chunks + c, groups, stride=sub), :] = q[:, cols]
        out_ref[:, r] = stage[...].reshape(groups, sub, LANES).astype(bf16)


def dispatch(ids_t, prob_t, tokens, cotangent, groups):
    sub = 2 * tokens.shape[1] // LANES
    return call(
        dispatch_body,
        jax.ShapeDtypeStruct((groups, CAP, sub, LANES), bf16),
        [pltpu.VMEM((groups * sub, LANES), f32)],
        2 * 2 * CAP * groups * tokens.size,
        4 * 2**20,
    )(ids_t, prob_t, tokens, cotangent)


def rows_body(got_ref, w_ref, x_ref, q_ref, da_ref, du_ref, h_ref, gate_ref, back_ref, stage, stage_back):
    groups, _, sub, _ = got_ref.shape
    chunks = sub // 2
    for r in range(CAP):
        stage[...] = got_ref[:, r].astype(f32).reshape(groups * sub, LANES)
        at = slice(r * groups, (r + 1) * groups)
        for c in range(chunks):
            cols = slice(c * LANES, (c + 1) * LANES)
            x_ref[at, cols] = stage[pl.ds(c, groups, stride=sub), :].astype(bf16)
            q_ref[at, cols] = stage[pl.ds(chunks + c, groups, stride=sub), :].astype(bf16)
    x = x_ref[...]
    a = mul(x, w_ref[0], NN)
    u = mul(x, w_ref[1], NN)
    dh = mul(q_ref[...], w_ref[2], NN)
    sig = jax.nn.sigmoid(a)
    silu = a * sig
    h = (silu * u).astype(bf16)
    da = (dh * u * (sig * (1.0 + a * (1.0 - sig)))).astype(bf16)
    du = (dh * silu).astype(bf16)
    h_ref[...] = h
    da_ref[...] = da
    du_ref[...] = du
    gate = jnp.sum(h.astype(f32) * dh, axis=1, keepdims=True)
    gate_ref[...] = jnp.broadcast_to(gate, gate_ref.shape)
    rows = mul(da, w_ref[0], NT) + mul(du, w_ref[1], NT)
    for r in range(CAP):
        for c in range(chunks):
            stage_back[pl.ds(r * chunks + c, groups, stride=CAP * chunks), :] = rows[
                r * groups : (r + 1) * groups, c * LANES : (c + 1) * LANES
            ]
    back_ref[...] = stage_back[...].reshape(back_ref.shape).astype(bf16)


def rows_products(got, whole):
    groups, _, sub, _ = got.shape
    width, hidden = whole.shape[1:]
    rows, chunks = groups * CAP, sub // 2
    like = jax.ShapeDtypeStruct
    return call(
        rows_body,
        (
            like((rows, width), bf16),
            like((rows, width), bf16),
            like((rows, hidden), bf16),
            like((rows, hidden), bf16),
            like((rows, hidden), bf16),
            like((rows, LANES), f32),
            like((groups, CAP, chunks, LANES), bf16),
        ),
        [
            pltpu.VMEM((groups * sub, LANES), f32),
            pltpu.VMEM((rows * chunks, LANES), f32),
        ],
        10 * rows * width * hidden,
        8 * 2**20,
    )(got, whole)


def grads_body(x_ref, q_ref, da_ref, du_ref, h_ref, out_ref):
    out_ref[0] = mul(x_ref[...], da_ref[...], TN).astype(bf16)
    out_ref[1] = mul(x_ref[...], du_ref[...], TN).astype(bf16)
    out_ref[2] = mul(q_ref[...], h_ref[...], TN).astype(bf16)


def weight_grads(x, q, da, du, h):
    rows, width = x.shape
    hidden = h.shape[1]
    return call(
        grads_body,
        jax.ShapeDtypeStruct((3, width, hidden), bf16),
        [],
        6 * rows * width * hidden,
        6 * 2**20,
    )(x, q, da, du, h)


def adam_body(grad_ref, one_ref, two_ref, gate_ref, out_ref, stage):
    slots, tiles, sub, _ = out_ref.shape
    lines = tiles * sub
    groups = gate_ref.shape[0] // CAP
    parts, blocks = grad_ref.shape[0] // slots, grad_ref.shape[1] // LANES
    for p in range(parts):
        at = slice(p * slots, (p + 1) * slots)
        grad = grad_ref[at, :].astype(f32)
        first_new = BETA_ONE * one_ref[at, :] + (1.0 - BETA_ONE) * grad
        second_new = BETA_TWO * two_ref[at, :] + (1.0 - BETA_TWO) * grad * grad
        first_hat = first_new * (1.0 / (1.0 - BETA_ONE**STEP))
        second_hat = second_new * (1.0 / (1.0 - BETA_TWO**STEP))
        update = first_hat / (jnp.sqrt(second_hat) + ADAM_EPS)
        for b in range(blocks):
            stage[pl.ds(p * blocks + b, slots, stride=lines), :] = update[:, b * LANES : (b + 1) * LANES]
    used = parts * blocks
    for r in range(CAP):
        stage[pl.ds(used + r, slots, stride=lines), :] = gate_ref[r * groups : (r + 1) * groups, :]
    for spare in range(used + CAP, lines):
        stage[pl.ds(spare, slots, stride=lines), :] = jnp.zeros((slots, LANES), f32)
    out_ref[...] = stage[...].reshape(out_ref.shape).astype(bf16)


def adam_update(gradient, moment_one, moment_two, gate, slots):
    lines = -(-(gradient.size // (slots * LANES) + CAP) // 8) * 8
    return call(
        adam_body,
        jax.ShapeDtypeStruct((slots, lines // 8, 8, LANES), bf16),
        [pltpu.VMEM((slots * lines, LANES), f32)],
        12 * gradient.size,
        12 * gradient.size,
    )(gradient, moment_one, moment_two, gate)


def swap_body(partner_ref, in_ref, out_ref):
    def step(d, carry):
        out_ref[d] = in_ref[partner_ref[d]]
        return carry

    lax.fori_loop(0, in_ref.shape[0], step, 0, unroll=8)


def swap_slots(partner, spread):
    vmem = pl.BlockSpec(memory_space=pltpu.VMEM)
    return pl.pallas_call(
        swap_body,
        out_shape=jax.ShapeDtypeStruct(spread.shape, spread.dtype),
        in_specs=[pl.BlockSpec(memory_space=pltpu.SMEM), vmem],
        out_specs=vmem,
        compiler_params=pltpu.CompilerParams(vmem_limit_bytes=48 * 2**20),
        cost_estimate=pl.CostEstimate(flops=0, bytes_accessed=4 * spread.size, transcendentals=0),
    )(partner, spread)


def collect_body(in_ref, out_ref, stage):
    slots, tiles, sub, _ = in_ref.shape
    lines = tiles * sub
    stage[...] = in_ref[...].astype(f32).reshape(slots * lines, LANES)
    parts, blocks = out_ref.shape[0] // slots, out_ref.shape[1] // LANES
    for p in range(parts):
        for b in range(blocks):
            out_ref[p * slots : (p + 1) * slots, b * LANES : (b + 1) * LANES] = stage[
                pl.ds(p * blocks + b, slots, stride=lines), :
            ].astype(bf16)


def collect(routed, shape):
    return call(
        collect_body,
        jax.ShapeDtypeStruct(shape, bf16),
        [pltpu.VMEM((routed.size // LANES, LANES), f32)],
        0,
        4 * routed.size,
    )(routed)


def combine_body(ids_ref, prob_ref, back_ref, gates_ref, tok_ref, gate_ref, stage, rows, gate_stage):
    groups, _, chunks, _ = back_ref.shape
    lines = CAP * chunks
    hots, picks = routing(ids_ref[...], groups)
    stage[...] = back_ref[...].astype(f32).reshape(groups * lines, LANES)
    for r in range(CAP):
        for c in range(chunks):
            rows[r * groups : (r + 1) * groups, c * LANES : (c + 1) * LANES] = stage[
                pl.ds(r * chunks + c, groups, stride=lines), :
            ].astype(bf16)
    tok_ref[...] = mul(jnp.concatenate(picks, axis=0).astype(bf16), rows[...], TN).astype(bf16)
    slots, tiles, sub, _ = gates_ref.shape
    gate_stage[...] = gates_ref[:, tiles - 1].astype(f32).reshape(slots * sub, LANES)
    first = sub - (tiles * sub - GATE_LINE)
    gate_at = sum(picks[r] * gate_stage[pl.ds(first + r, groups, stride=sub), :] for r in range(CAP))
    for k in range(2):
        total = jnp.sum(jnp.where(hots[k], gate_at, 0.0), axis=0, keepdims=True)
        gate_ref[k : k + 1, :] = total / prob_ref[k : k + 1, :].astype(f32)


GATE_LINE = 18


def combine(ids_t, prob_t, back, spread):
    groups, _, chunks, _ = back.shape
    tok_count = ids_t.shape[1]
    width = chunks * LANES
    return call(
        combine_body,
        (
            jax.ShapeDtypeStruct((tok_count, width), bf16),
            jax.ShapeDtypeStruct((2, tok_count), f32),
        ),
        [
            pltpu.VMEM((groups * CAP * chunks, LANES), f32),
            pltpu.VMEM((groups * CAP, width), bf16),
            pltpu.VMEM((spread.shape[0] * 8, LANES), f32),
        ],
        2 * CAP * groups * tok_count * width,
        4 * 2**20,
    )(ids_t, prob_t, back, spread)


def on_device(
    tokens,
    cotangent,
    route_ids,
    gate_prob,
    swap_partner,
    expert_weights,
    first_moment,
    second_moment,
):
    groups = lax.axis_size("expert")
    hidden = expert_weights.shape[3]
    flat = (-1, hidden)
    ids_t, prob_t = route_ids.T, gate_prob.T

    whole = lax.all_gather(expert_weights, "dp", axis=2, tiled=True)[0]
    got = exchange(dispatch(ids_t, prob_t, tokens, cotangent, groups))
    x, q, da, du, h, gate, returned = rows_products(got, whole)
    back = exchange(returned)
    partial = weight_grads(x, q, da, du, h)
    gradient = lax.psum_scatter(partial, "dp", scatter_dimension=1, tiled=True)
    staged = adam_update(
        gradient.reshape(flat), first_moment.reshape(flat), second_moment.reshape(flat), gate, groups
    )
    back, staged = lax.optimization_barrier((back, staged))
    spread = exchange(staged)
    routed = exchange(swap_slots(swap_partner, spread))
    token_grad, gate_grad = combine(ids_t, prob_t, back, spread)
    update = collect(routed, gradient.reshape(flat).shape)
    return (token_grad, gate_grad.T.astype(bf16), update.reshape(expert_weights.shape))


def solution(mesh):
    placed = (
        P(("expert", "dp"), None),
        P(("expert", "dp"), None),
        P(("expert", "dp"), None),
        P(("expert", "dp"), None),
        P(),
        P("expert", None, "dp", None),
        P("expert", None, "dp", None),
        P("expert", None, "dp", None),
    )
    return jax.shard_map(
        on_device,
        mesh=mesh,
        in_specs=placed,
        out_specs=(
            P(("expert", "dp"), None),
            P(("expert", "dp"), None),
            P("expert", None, "dp", None),
        ),
        check_vma=False,
    )
```

```python
import functools

import jax
import jax.numpy as jnp
from jax import lax
from jax.experimental import pallas as pl
from jax.experimental.pallas import tpu as pltpu
from jax.sharding import PartitionSpec as P

STEP = 100
BETA_ONE = 0.9
BETA_TWO = 0.95
ADAM_EPS = 1e-08
CAP = 3
LANES = 128
f32, bf16 = jnp.float32, jnp.bfloat16

NN = (((1,), (0,)), ((), ()))
NT = (((1,), (1,)), ((), ()))
TN = (((0,), (0,)), ((), ()))


def mul(a, b, dims):
    return lax.dot_general(a, b, dims, preferred_element_type=f32)


def call(body, outs, scratch, flops, moved):
    return pl.pallas_call(
        body,
        out_shape=outs,
        scratch_shapes=scratch,
        compiler_params=pltpu.CompilerParams(vmem_limit_bytes=48 * 2**20),
        cost_estimate=pl.CostEstimate(flops=flops, bytes_accessed=moved, transcendentals=0),
    )


def exchange(x):
    return lax.all_to_all(x, "expert", split_axis=0, concat_axis=0, tiled=True)


def routing(ids, groups):
    tok_count = ids.shape[1]
    expert = lax.broadcasted_iota(jnp.int32, (groups, tok_count), 0)
    hots = [ids[k : k + 1, :] == expert for k in range(2)]
    named = jnp.where(hots[0] | hots[1], 1.0, 0.0)
    before = lax.broadcasted_iota(jnp.int32, (tok_count, tok_count), 0)
    after = lax.broadcasted_iota(jnp.int32, (tok_count, tok_count), 1)
    earlier = jnp.where(before < after, 1.0, 0.0).astype(bf16)
    rank = mul(named.astype(bf16), earlier, NN)
    return hots, [jnp.where(rank == r, named, 0.0) for r in range(CAP)]


def dispatch_body(ids_ref, prob_ref, tok_ref, cot_ref, out_ref, stage):
    groups, _, sub, _ = out_ref.shape
    chunks = sub // 2
    hots, picks = routing(ids_ref[...], groups)
    prob = prob_ref[...].astype(f32)
    prob_at = jnp.where(hots[0], prob[0:1, :], jnp.where(hots[1], prob[1:2, :], 0.0))
    for r in range(CAP):
        x = mul(picks[r].astype(bf16), tok_ref[...], NN)
        q = mul((picks[r] * prob_at).astype(bf16), cot_ref[...], NN)
        for c in range(chunks):
            cols = slice(c * LANES, (c + 1) * LANES)
            stage[pl.ds(c, groups, stride=sub), :] = x[:, cols]
            stage[pl.ds(chunks + c, groups, stride=sub), :] = q[:, cols]
        out_ref[:, r] = stage[...].reshape(groups, sub, LANES).astype(bf16)


def dispatch(ids_t, prob_t, tokens, cotangent, groups):
    sub = 2 * tokens.shape[1] // LANES
    return call(
        dispatch_body,
        jax.ShapeDtypeStruct((groups, CAP, sub, LANES), bf16),
        [pltpu.VMEM((groups * sub, LANES), f32)],
        2 * 2 * CAP * groups * tokens.size,
        4 * 2**20,
    )(ids_t, prob_t, tokens, cotangent)


def rows_body(got_ref, w_ref, x_ref, q_ref, da_ref, du_ref, h_ref, back_ref, rest_ref, last_ref, stage):
    groups, _, sub, _ = got_ref.shape
    chunks = sub // 2
    for r in range(CAP):
        stage[...] = got_ref[:, r].astype(f32).reshape(groups * sub, LANES)
        at = slice(r * groups, (r + 1) * groups)
        for c in range(chunks):
            cols = slice(c * LANES, (c + 1) * LANES)
            x_ref[at, cols] = stage[pl.ds(c, groups, stride=sub), :].astype(bf16)
            q_ref[at, cols] = stage[pl.ds(chunks + c, groups, stride=sub), :].astype(bf16)
    x = x_ref[...]
    a = mul(x, w_ref[0], NN)
    u = mul(x, w_ref[1], NN)
    dh = mul(q_ref[...], w_ref[2], NN)
    sig = jax.nn.sigmoid(a)
    silu = a * sig
    h = (silu * u).astype(bf16)
    da = (dh * u * (sig * (1.0 + a * (1.0 - sig)))).astype(bf16)
    du = (dh * silu).astype(bf16)
    h_ref[...] = h
    da_ref[...] = da
    du_ref[...] = du
    gate = jnp.sum(h.astype(f32) * dh, axis=1, keepdims=True)
    rows = mul(da, w_ref[0], NT) + mul(du, w_ref[1], NT)
    for r in range(CAP - 1):
        for c in range(chunks):
            stage[pl.ds(r * chunks + c, groups, stride=sub), :] = rows[
                r * groups : (r + 1) * groups, c * LANES : (c + 1) * LANES
            ]
    back_ref[...] = stage[...].reshape(back_ref.shape).astype(bf16)
    first = rest_ref.shape[1]
    left = rows[(CAP - 1) * groups :, :]
    rest_ref[...] = left[:, :first].astype(bf16)
    extra = [left[:, c : c + LANES] for c in range(first, chunks * LANES, LANES)]
    extra += [jnp.broadcast_to(gate[r * groups : (r + 1) * groups], (groups, LANES)) for r in range(CAP)]
    free = first // LANES
    for line in range(8):
        at = line - (8 - free)
        value = extra[at] if 0 <= at < len(extra) else jnp.zeros((groups, LANES), f32)
        stage[pl.ds(line, groups, stride=8), :] = value
    last_ref[...] = stage[: groups * 8, :].reshape(groups, 8, LANES).astype(bf16)


def rows_products(got, whole, free):
    groups, _, sub, _ = got.shape
    width, hidden = whole.shape[1:]
    rows, chunks = groups * CAP, sub // 2
    like = jax.ShapeDtypeStruct
    return call(
        rows_body,
        (
            like((rows, width), bf16),
            like((rows, width), bf16),
            like((rows, hidden), bf16),
            like((rows, hidden), bf16),
            like((rows, hidden), bf16),
            like((groups, CAP - 1, chunks, LANES), bf16),
            like((groups, free * LANES), bf16),
            like((groups, 8, LANES), bf16),
        ),
        [pltpu.VMEM((groups * sub, LANES), f32)],
        10 * rows * width * hidden,
        8 * 2**20,
    )(got, whole)


def grads_body(core_ref, x_ref, q_ref, da_ref, du_ref, h_ref, keep_ref, send_ref):
    halves, _, depth, _ = keep_ref.shape
    for out_ref, core in ((send_ref, 1 - core_ref[0]), (keep_ref, core_ref[0])):
        for half in range(halves):
            cols = pl.ds(pl.multiple_of((half * 2 + core) * depth, depth), depth)
            out_ref[half, 0] = mul(x_ref[:, cols], da_ref[...], TN).astype(bf16)
            out_ref[half, 1] = mul(x_ref[:, cols], du_ref[...], TN).astype(bf16)
            out_ref[half, 2] = mul(q_ref[:, cols], h_ref[...], TN).astype(bf16)


def weight_grads(core, x, q, da, du, h):
    rows, width = x.shape
    hidden = h.shape[1]
    vmem = pl.BlockSpec(memory_space=pltpu.VMEM)
    half = jax.ShapeDtypeStruct((2, 3, width // 4, hidden), bf16)
    return pl.pallas_call(
        grads_body,
        out_shape=(half, half),
        in_specs=[pl.BlockSpec(memory_space=pltpu.SMEM)] + [vmem] * 5,
        out_specs=(vmem, vmem),
        compiler_params=pltpu.CompilerParams(vmem_limit_bytes=48 * 2**20),
        cost_estimate=pl.CostEstimate(
            flops=6 * rows * width * hidden, bytes_accessed=6 * 2**20, transcendentals=0
        ),
    )(core, x, q, da, du, h)


def pair_body(side_ref, keep_ref, got_ref, own_ref, send_ref):
    side = side_ref[0]
    send_ref[...] = (keep_ref[1 - side].astype(f32) + got_ref[1 - side].astype(f32)).astype(bf16)
    own_ref[...] = keep_ref[side].astype(f32) + got_ref[side].astype(f32)


def pair_sum(side, keep, got):
    vmem = pl.BlockSpec(memory_space=pltpu.VMEM)
    return pl.pallas_call(
        pair_body,
        out_shape=(
            jax.ShapeDtypeStruct(keep.shape[1:], f32),
            jax.ShapeDtypeStruct(keep.shape[1:], bf16),
        ),
        in_specs=[pl.BlockSpec(memory_space=pltpu.SMEM), vmem, vmem],
        out_specs=(vmem, vmem),
        compiler_params=pltpu.CompilerParams(vmem_limit_bytes=48 * 2**20),
        cost_estimate=pl.CostEstimate(flops=keep.size, bytes_accessed=5 * keep.size, transcendentals=0),
    )(side, keep, got)


def adam_body(own_ref, other_ref, one_ref, two_ref, rest_ref, out_ref, stage):
    slots, tiles, sub, _ = out_ref.shape
    lines = tiles * sub
    parts, blocks = own_ref.shape[0] // slots, own_ref.shape[1] // LANES
    for p in range(parts):
        at = slice(p * slots, (p + 1) * slots)
        grad = own_ref[at, :] + other_ref[at, :].astype(f32)
        first_new = BETA_ONE * one_ref[at, :] + (1.0 - BETA_ONE) * grad
        second_new = BETA_TWO * two_ref[at, :] + (1.0 - BETA_TWO) * grad * grad
        first_hat = first_new * (1.0 / (1.0 - BETA_ONE**STEP))
        second_hat = second_new * (1.0 / (1.0 - BETA_TWO**STEP))
        update = first_hat / (jnp.sqrt(second_hat) + ADAM_EPS)
        for b in range(blocks):
            stage[pl.ds(p * blocks + b, slots, stride=lines), :] = update[:, b * LANES : (b + 1) * LANES]
    used = parts * blocks
    for c in range(lines - used):
        stage[pl.ds(used + c, slots, stride=lines), :] = rest_ref[:, c * LANES : (c + 1) * LANES].astype(f32)
    out_ref[...] = stage[...].reshape(out_ref.shape).astype(bf16)


def adam_update(own, other, moment_one, moment_two, rest, slots, lines):
    return call(
        adam_body,
        jax.ShapeDtypeStruct((slots, lines // 8, 8, LANES), bf16),
        [pltpu.VMEM((slots * lines, LANES), f32)],
        12 * own.size,
        14 * own.size,
    )(own, other, moment_one, moment_two, rest)


def swap_body(free, partner_ref, in_ref, last_ref, out_ref):
    slots, tiles, sub, _ = in_ref.shape
    update = lax.broadcasted_iota(jnp.int32, (sub, LANES), 0) < sub - free

    def step(d, carry):
        source = partner_ref[d]
        for t in range(tiles - 1):
            out_ref[d, t] = in_ref[source, t]
        moved = in_ref[source, tiles - 1].astype(f32)
        out_ref[d, tiles - 1] = jnp.where(update, moved, last_ref[d].astype(f32)).astype(bf16)
        return carry

    lax.fori_loop(0, slots, step, 0, unroll=8)


def swap_slots(partner, spread, last, free):
    vmem = pl.BlockSpec(memory_space=pltpu.VMEM)
    return pl.pallas_call(
        functools.partial(swap_body, free),
        out_shape=jax.ShapeDtypeStruct(spread.shape, spread.dtype),
        in_specs=[pl.BlockSpec(memory_space=pltpu.SMEM), vmem, vmem],
        out_specs=vmem,
        compiler_params=pltpu.CompilerParams(vmem_limit_bytes=48 * 2**20),
        cost_estimate=pl.CostEstimate(flops=0, bytes_accessed=4 * spread.size, transcendentals=0),
    )(partner, spread, last)


def finish_body(free, ids_ref, prob_ref, back_ref, spread_ref, routed_ref, tok_ref, gate_ref, out_ref, stage, rows):
    groups, ranks, chunks, _ = back_ref.shape
    slots, tiles, sub, _ = routed_ref.shape
    lines = tiles * sub
    parts, blocks = out_ref.shape[0] // slots, out_ref.shape[1] // LANES
    hots, picks = routing(ids_ref[...], groups)
    held = groups * ranks * chunks
    stage[:held, :] = back_ref[...].astype(f32).reshape(held, LANES)
    for r in range(ranks):
        for c in range(chunks):
            rows[r * groups : (r + 1) * groups, c * LANES : (c + 1) * LANES] = stage[
                pl.ds(r * chunks + c, groups, stride=ranks * chunks), :
            ].astype(bf16)
    at = slice(ranks * groups, (ranks + 1) * groups)
    stage[: groups * sub, :] = spread_ref[:, tiles - 1].astype(f32).reshape(groups * sub, LANES)
    for c in range(free):
        rows[at, c * LANES : (c + 1) * LANES] = stage[pl.ds(sub - free + c, groups, stride=sub), :].astype(bf16)
    stage[...] = routed_ref[...].astype(f32).reshape(slots * lines, LANES)
    for p in range(parts):
        for b in range(blocks):
            out_ref[p * slots : (p + 1) * slots, b * LANES : (b + 1) * LANES] = stage[
                pl.ds(p * blocks + b, slots, stride=lines), :
            ].astype(bf16)
    extra = [stage[pl.ds(lines - free + c, groups, stride=lines), :] for c in range(free)]
    for c in range(free, chunks):
        rows[at, c * LANES : (c + 1) * LANES] = extra[c - free].astype(bf16)
    tok_ref[...] = mul(jnp.concatenate(picks, axis=0).astype(bf16), rows[...], TN).astype(bf16)
    gate_at = sum(picks[r] * extra[chunks - free + r] for r in range(CAP))
    for k in range(2):
        total = jnp.sum(jnp.where(hots[k], gate_at, 0.0), axis=0, keepdims=True)
        gate_ref[k : k + 1, :] = total / prob_ref[k : k + 1, :].astype(f32)


def finish(ids_t, prob_t, back, spread, routed, shape, free):
    groups, _, chunks, _ = back.shape
    tok_count = ids_t.shape[1]
    width = chunks * LANES
    return call(
        functools.partial(finish_body, free),
        (
            jax.ShapeDtypeStruct((tok_count, width), bf16),
            jax.ShapeDtypeStruct((2, tok_count), f32),
            jax.ShapeDtypeStruct(shape, bf16),
        ),
        [
            pltpu.VMEM((routed.size // LANES, LANES), f32),
            pltpu.VMEM((groups * CAP, width), bf16),
        ],
        2 * CAP * groups * tok_count * width,
        4 * 2**20,
    )(ids_t, prob_t, back, spread, routed)


def on_device(
    tokens,
    cotangent,
    route_ids,
    gate_prob,
    swap_partner,
    expert_weights,
    first_moment,
    second_moment,
):
    groups = lax.axis_size("expert")
    hidden = expert_weights.shape[3]
    flat = (expert_weights.size // hidden, hidden)
    ids_t, prob_t = route_ids.T, gate_prob.T
    replica = lax.axis_index("dp")
    core, side = (replica % 2).reshape(1), (replica // 2).reshape(1)
    used = expert_weights.size // (groups * LANES)
    lines = -(-used // 8) * 8
    free = lines - used

    whole = lax.all_gather(expert_weights, "dp", axis=2, tiled=True)[0]
    got = exchange(dispatch(ids_t, prob_t, tokens, cotangent, groups))
    x, q, da, du, h, returned, rest, last = rows_products(got, whole, free)
    back = exchange(returned)
    keep, sent = weight_grads(core, x, q, da, du, h)
    own, sent = pair_sum(side, keep, lax.ppermute(sent, "dp", [(0, 1), (1, 0), (2, 3), (3, 2)]))
    other = lax.ppermute(sent, "dp", [(0, 2), (2, 0), (1, 3), (3, 1)])
    staged = adam_update(
        own.reshape(flat),
        other.reshape(flat),
        first_moment.reshape(flat),
        second_moment.reshape(flat),
        rest,
        groups,
        lines,
    )
    back, staged = lax.optimization_barrier((back, staged))
    spread = exchange(staged)
    routed = exchange(swap_slots(swap_partner, spread, last, free))
    token_grad, gate_grad, update = finish(ids_t, prob_t, back, spread, routed, flat, free)
    return (token_grad, gate_grad.T.astype(bf16), update.reshape(expert_weights.shape))


def solution(mesh):
    placed = (
        P(("expert", "dp"), None),
        P(("expert", "dp"), None),
        P(("expert", "dp"), None),
        P(("expert", "dp"), None),
        P(),
        P("expert", None, "dp", None),
        P("expert", None, "dp", None),
        P("expert", None, "dp", None),
    )
    return jax.shard_map(
        on_device,
        mesh=mesh,
        in_specs=placed,
        out_specs=(
            P(("expert", "dp"), None),
            P(("expert", "dp"), None),
            P("expert", None, "dp", None),
        ),
        check_vma=False,
    )
```

```python
import jax
import jax.numpy as jnp
from jax import lax
from jax.experimental import pallas as pl
from jax.experimental.pallas import tpu as pltpu
from jax.sharding import PartitionSpec as P

STEP = 100
BETA_ONE = 0.9
BETA_TWO = 0.95
ADAM_EPS = 1e-08
CAP = 3
LANES = 128
SLOTS = 128
f32, bf16 = jnp.float32, jnp.bfloat16

NN = (((1,), (0,)), ((), ()))
NT = (((1,), (1,)), ((), ()))
TN = (((0,), (0,)), ((), ()))


def mul(a, b, dims):
    return lax.dot_general(a, b, dims, preferred_element_type=f32)


def call(body, outs, scratch, flops, moved, ins=None, limit=16):
    return pl.pallas_call(
        body,
        out_shape=outs,
        **({} if ins is None else {'in_specs': ins}),
        scratch_shapes=scratch,
        compiler_params=pltpu.CompilerParams(vmem_limit_bytes=limit * 2**20),
        cost_estimate=pl.CostEstimate(flops=flops, bytes_accessed=moved, transcendentals=0),
    )


def exchange(x):
    return lax.all_to_all(x, "expert", split_axis=0, concat_axis=0, tiled=True)


def routing(ids, groups):
    tok_count = ids.shape[1]
    expert = lax.broadcasted_iota(jnp.int32, (groups, tok_count), 0)
    hots = [ids[k : k + 1, :] == expert for k in range(2)]
    named = jnp.where(hots[0] | hots[1], 1.0, 0.0)
    before = lax.broadcasted_iota(jnp.int32, (tok_count, tok_count), 0)
    after = lax.broadcasted_iota(jnp.int32, (tok_count, tok_count), 1)
    earlier = jnp.where(before < after, 1.0, 0.0).astype(bf16)
    rank = mul(named.astype(bf16), earlier, NN)
    return hots, [jnp.where(rank == r, named, 0.0) for r in range(CAP)]


def dispatch_body(ids_hbm, prob_hbm, tok_hbm, cot_hbm, out_ref, ids_ref, prob_ref, tok_ref, cot_ref, stage, sems):
    pairs = ((ids_hbm, ids_ref), (prob_hbm, prob_ref), (tok_hbm, tok_ref), (cot_hbm, cot_ref))
    copies = [pltpu.make_async_copy(src, dst, sems.at[i]) for i, (src, dst) in enumerate(pairs)]
    for copy in copies:
        copy.start()
    groups, _, sub, _ = out_ref.shape
    chunks = sub // 2
    copies[0].wait()
    hots, picks = routing(ids_ref[...], groups)
    copies[1].wait()
    prob = prob_ref[...].astype(f32)
    prob_at = jnp.where(hots[0], prob[0:1, :], jnp.where(hots[1], prob[1:2, :], 0.0))
    copies[2].wait()
    copies[3].wait()
    for r in range(CAP):
        x = mul(picks[r].astype(bf16), tok_ref[...], NN)
        q = mul((picks[r] * prob_at).astype(bf16), cot_ref[...], NN)
        for c in range(chunks):
            cols = slice(c * LANES, (c + 1) * LANES)
            stage[pl.ds(c, groups, stride=sub), :] = x[:, cols]
            stage[pl.ds(chunks + c, groups, stride=sub), :] = q[:, cols]
        out_ref[:, r] = stage[...].reshape(groups, sub, LANES).astype(bf16)


def dispatch(ids_t, prob_t, tokens, cotangent, groups):
    sub = 2 * tokens.shape[1] // LANES
    return call(
        dispatch_body,
        jax.ShapeDtypeStruct((groups, CAP, sub, LANES), bf16),
        [pltpu.VMEM(a.shape, a.dtype) for a in (ids_t, prob_t, tokens, cotangent)]
        + [pltpu.VMEM((groups * sub, LANES), f32), pltpu.SemaphoreType.DMA((4,))],
        2 * 2 * CAP * groups * tokens.size,
        4 * 2**20,
        [pl.BlockSpec(memory_space=pltpu.HBM)] * 4,
    )(ids_t, prob_t, tokens, cotangent)


def expert_body(core_ref, got_ref, w_ref, back_ref, keep_ref, send_ref, x_ref, q_ref, da_ref, du_ref, h_ref, stage, stage_back):
    groups, _, sub, _ = got_ref.shape
    chunks = sub // 2
    for r in range(CAP):
        stage[...] = got_ref[:, r].astype(f32).reshape(groups * sub, LANES)
        at = slice(r * groups, (r + 1) * groups)
        for c in range(chunks):
            cols = slice(c * LANES, (c + 1) * LANES)
            x_ref[at, cols] = stage[pl.ds(c, groups, stride=sub), :].astype(bf16)
            q_ref[at, cols] = stage[pl.ds(chunks + c, groups, stride=sub), :].astype(bf16)
    x = x_ref[...]
    a = mul(x, w_ref[0], NN)
    u = mul(x, w_ref[1], NN)
    dh = mul(q_ref[...], w_ref[2], NN)
    sig = jax.nn.sigmoid(a)
    silu = a * sig
    h = (silu * u).astype(bf16)
    da = (dh * u * (sig * (1.0 + a * (1.0 - sig)))).astype(bf16)
    du = (dh * silu).astype(bf16)
    h_ref[...] = h
    da_ref[...] = da
    du_ref[...] = du
    gate = jnp.sum(h.astype(f32) * dh, axis=1, keepdims=True)
    rows = mul(da, w_ref[0], NT) + mul(du, w_ref[1], NT)
    lines = stage_back.shape[0] // groups
    for r in range(CAP):
        at = slice(r * groups, (r + 1) * groups)
        for c in range(chunks):
            stage_back[pl.ds(r * chunks + c, groups, stride=lines), :] = rows[at, c * LANES : (c + 1) * LANES]
        stage_back[pl.ds(CAP * chunks + r, groups, stride=lines), :] = jnp.broadcast_to(gate[at], (groups, LANES))
    for spare in range(CAP * (chunks + 1), lines):
        stage_back[pl.ds(spare, groups, stride=lines), :] = jnp.zeros((groups, LANES), f32)
    back_ref[...] = stage_back[...].reshape(back_ref.shape).astype(bf16)
    halves, _, depth, _ = keep_ref.shape
    for out_ref, core in ((send_ref, 1 - core_ref[0]), (keep_ref, core_ref[0])):
        for half in range(halves):
            cols = pl.ds(pl.multiple_of((half * 2 + core) * depth, depth), depth)
            out_ref[half, 0] = mul(x_ref[:, cols], da_ref[...], TN).astype(bf16)
            out_ref[half, 1] = mul(x_ref[:, cols], du_ref[...], TN).astype(bf16)
            out_ref[half, 2] = mul(q_ref[:, cols], h_ref[...], TN).astype(bf16)


def expert_step(core, got, whole):
    groups, _, sub, _ = got.shape
    width, hidden = whole.shape[1:]
    rows, chunks = groups * CAP, sub // 2
    lines = -(-CAP * (chunks + 1) // 2) * 2
    like = jax.ShapeDtypeStruct
    half = like((2, 3, width // 4, hidden), bf16)
    vmem = pl.BlockSpec(memory_space=pltpu.VMEM)
    return call(
        expert_body,
        (like((groups * lines // 8, 8, LANES), bf16), half, half),
        [pltpu.VMEM((rows, width), bf16)] * 2
        + [pltpu.VMEM((rows, hidden), bf16)] * 3
        + [pltpu.VMEM((groups * sub, LANES), f32), pltpu.VMEM((groups * lines, LANES), f32)],
        16 * rows * width * hidden,
        12 * 2**20,
        [pl.BlockSpec(memory_space=pltpu.SMEM), vmem, vmem],
        30,
    )(core, got, whole)


def pair_body(side_ref, keep_ref, got_ref, own_ref, send_ref):
    side = side_ref[0]
    send_ref[...] = (keep_ref[1 - side].astype(f32) + got_ref[1 - side].astype(f32)).astype(bf16)
    own_ref[...] = keep_ref[side].astype(f32) + got_ref[side].astype(f32)


def pair_sum(side, keep, got):
    vmem = pl.BlockSpec(memory_space=pltpu.VMEM)
    return pl.pallas_call(
        pair_body,
        out_shape=(
            jax.ShapeDtypeStruct(keep.shape[1:], f32),
            jax.ShapeDtypeStruct(keep.shape[1:], bf16),
        ),
        in_specs=[pl.BlockSpec(memory_space=pltpu.SMEM), vmem, vmem],
        out_specs=(vmem, vmem),
        compiler_params=pltpu.CompilerParams(vmem_limit_bytes=16 * 2**20),
        cost_estimate=pl.CostEstimate(flops=keep.size, bytes_accessed=5 * keep.size, transcendentals=0),
    )(side, keep, got)


def adam_body(own_ref, other_ref, one_ref, two_ref, out_ref, stage):
    blocks = own_ref.shape[1] // LANES
    lines = own_ref.shape[0] * blocks // SLOTS
    for p in range(lines // blocks):
        at = slice(p * SLOTS, (p + 1) * SLOTS)
        grad = own_ref[at, :] + other_ref[at, :].astype(f32)
        first_new = BETA_ONE * one_ref[at, :] + (1.0 - BETA_ONE) * grad
        second_new = BETA_TWO * two_ref[at, :] + (1.0 - BETA_TWO) * grad * grad
        first_hat = first_new * (1.0 / (1.0 - BETA_ONE**STEP))
        second_hat = second_new * (1.0 / (1.0 - BETA_TWO**STEP))
        update = first_hat / (jnp.sqrt(second_hat) + ADAM_EPS)
        for b in range(blocks):
            stage[pl.ds(p * blocks + b, SLOTS, stride=lines), :] = update[:, b * LANES : (b + 1) * LANES]
    out_ref[...] = stage[...].reshape(out_ref.shape).astype(bf16)


def adam_update(own, other, moment_one, moment_two):
    return call(
        adam_body,
        jax.ShapeDtypeStruct((own.size // (8 * LANES), 8, LANES), bf16),
        [pltpu.VMEM((own.size // LANES, LANES), f32)],
        12 * own.size,
        14 * own.size,
    )(own, other, moment_one, moment_two)


def swap_body(partner_ref, in_ref, out_ref):
    def step(d, carry):
        out_ref[d] = in_ref[partner_ref[d]]
        return carry

    lax.fori_loop(0, in_ref.shape[0], step, 0, unroll=8)


def swap_slots(partner, spread):
    vmem = pl.BlockSpec(memory_space=pltpu.VMEM)
    return call(
        swap_body,
        jax.ShapeDtypeStruct(spread.shape, spread.dtype),
        [],
        0,
        4 * spread.size,
        [pl.BlockSpec(memory_space=pltpu.SMEM), vmem],
    )(partner, spread)


def collect_body(in_ref, out_ref, stage):
    stage[...] = in_ref[...].astype(f32).reshape(stage.shape)
    blocks = out_ref.shape[1] // LANES
    lines = stage.shape[0] // SLOTS
    for p in range(lines // blocks):
        for b in range(blocks):
            out_ref[p * SLOTS : (p + 1) * SLOTS, b * LANES : (b + 1) * LANES] = stage[
                pl.ds(p * blocks + b, SLOTS, stride=lines), :
            ].astype(bf16)


def collect(routed, shape):
    return call(
        collect_body,
        jax.ShapeDtypeStruct(shape, bf16),
        [pltpu.VMEM((routed.size // LANES, LANES), f32)],
        0,
        4 * routed.size,
    )(routed)


def combine_body(ids_ref, prob_ref, back_ref, tok_ref, gate_ref, stage, rows):
    groups, chunks = rows.shape[0] // CAP, rows.shape[1] // LANES
    lines = stage.shape[0] // groups
    hots, picks = routing(ids_ref[...], groups)
    stage[...] = back_ref[...].astype(f32).reshape(stage.shape)
    for r in range(CAP):
        for c in range(chunks):
            rows[r * groups : (r + 1) * groups, c * LANES : (c + 1) * LANES] = stage[
                pl.ds(r * chunks + c, groups, stride=lines), :
            ].astype(bf16)
    tok_ref[...] = mul(jnp.concatenate(picks, axis=0).astype(bf16), rows[...], TN).astype(bf16)
    gate_at = sum(picks[r] * stage[pl.ds(CAP * chunks + r, groups, stride=lines), :] for r in range(CAP))
    for k in range(2):
        total = jnp.sum(jnp.where(hots[k], gate_at, 0.0), axis=0, keepdims=True)
        gate_ref[k : k + 1, :] = total / prob_ref[k : k + 1, :].astype(f32)


def combine(ids_t, prob_t, back, width, groups):
    tok_count = ids_t.shape[1]
    return call(
        combine_body,
        (
            jax.ShapeDtypeStruct((tok_count, width), bf16),
            jax.ShapeDtypeStruct((2, tok_count), f32),
        ),
        [
            pltpu.VMEM((back.size // LANES, LANES), f32),
            pltpu.VMEM((groups * CAP, width), bf16),
        ],
        2 * CAP * groups * tok_count * width,
        4 * 2**20,
    )(ids_t, prob_t, back)


def on_device(
    tokens,
    cotangent,
    route_ids,
    gate_prob,
    swap_partner,
    expert_weights,
    first_moment,
    second_moment,
):
    groups = lax.axis_size("expert")
    hidden = expert_weights.shape[3]
    flat = (expert_weights.size // hidden, hidden)
    ids_t, prob_t = route_ids.T, gate_prob.T
    replica = lax.axis_index("dp")
    core, side = (replica % 2).reshape(1), (replica // 2).reshape(1)
    tiles, pairs = (-1, 8, LANES), (groups, -1, 2, LANES)

    whole = lax.all_gather(expert_weights, "dp", axis=2, tiled=True)[0]
    got = exchange(dispatch(ids_t, prob_t, tokens, cotangent, groups))
    returned, keep, sent = expert_step(core, got, whole)
    own, sent = pair_sum(side, keep, lax.ppermute(sent, "dp", [(0, 1), (1, 0), (2, 3), (3, 2)]))
    back = exchange(returned.reshape(pairs))
    other = lax.ppermute(sent, "dp", [(0, 2), (2, 0), (1, 3), (3, 1)])
    staged = adam_update(
        own.reshape(flat), other.reshape(flat), first_moment.reshape(flat), second_moment.reshape(flat)
    )
    back, staged = lax.optimization_barrier((back, staged))
    spread = exchange(staged.reshape(pairs))
    routed = exchange(swap_slots(swap_partner, spread))
    token_grad, gate_grad = combine(ids_t, prob_t, back.reshape(tiles), tokens.shape[1], groups)
    update = collect(routed.reshape(tiles), flat)
    return (token_grad, gate_grad.T.astype(bf16), update.reshape(expert_weights.shape))


def solution(mesh):
    placed = (
        P(("expert", "dp"), None),
        P(("expert", "dp"), None),
        P(("expert", "dp"), None),
        P(("expert", "dp"), None),
        P(),
        P("expert", None, "dp", None),
        P("expert", None, "dp", None),
        P("expert", None, "dp", None),
    )
    return jax.shard_map(
        on_device,
        mesh=mesh,
        in_specs=placed,
        out_specs=(
            P(("expert", "dp"), None),
            P(("expert", "dp"), None),
            P("expert", None, "dp", None),
        ),
        check_vma=False,
    )
```

```python
import jax
import jax.numpy as jnp
from jax import lax
from jax.experimental import pallas as pl
from jax.experimental.pallas import tpu as pltpu
from jax.sharding import PartitionSpec as P

STEP = 100
BETA_ONE = 0.9
BETA_TWO = 0.95
ADAM_EPS = 1e-08
CAP = 3
LANES = 128
SLOTS = 128
BESIDE = [(0, 1), (1, 0), (2, 3), (3, 2)]
ACROSS = [(0, 2), (2, 0), (1, 3), (3, 1)]
f32, bf16 = jnp.float32, jnp.bfloat16

NN = (((1,), (0,)), ((), ()))
NT = (((1,), (1,)), ((), ()))
TN = (((0,), (0,)), ((), ()))


def mul(a, b, dims):
    return lax.dot_general(a, b, dims, preferred_element_type=f32)


def call(body, outs, scratch, flops, moved, ins=None, limit=16):
    return pl.pallas_call(
        body,
        out_shape=outs,
        **({} if ins is None else {'in_specs': ins}),
        scratch_shapes=scratch,
        compiler_params=pltpu.CompilerParams(vmem_limit_bytes=limit * 2**20),
        cost_estimate=pl.CostEstimate(flops=flops, bytes_accessed=moved, transcendentals=0),
    )


def exchange(x):
    return lax.all_to_all(x, "expert", split_axis=0, concat_axis=0, tiled=True)


def routing(ids, groups):
    tok_count = ids.shape[1]
    expert = lax.broadcasted_iota(jnp.int32, (groups, tok_count), 0)
    hots = [ids[k : k + 1, :] == expert for k in range(2)]
    named = jnp.where(hots[0] | hots[1], 1.0, 0.0)
    before = lax.broadcasted_iota(jnp.int32, (tok_count, tok_count), 0)
    after = lax.broadcasted_iota(jnp.int32, (tok_count, tok_count), 1)
    earlier = jnp.where(before < after, 1.0, 0.0).astype(bf16)
    rank = mul(named.astype(bf16), earlier, NN)
    return hots, [jnp.where(rank == r, named, 0.0) for r in range(CAP)]


def dispatch_body(ids_hbm, prob_hbm, tok_hbm, cot_hbm, out_ref, ids_ref, prob_ref, tok_ref, cot_ref, stage, sems):
    pairs = ((ids_hbm, ids_ref), (prob_hbm, prob_ref), (tok_hbm, tok_ref), (cot_hbm, cot_ref))
    copies = [pltpu.make_async_copy(src, dst, sems.at[i]) for i, (src, dst) in enumerate(pairs)]
    for copy in copies:
        copy.start()
    groups, _, sub, _ = out_ref.shape
    chunks = sub // 2
    copies[0].wait()
    hots, picks = routing(ids_ref[...], groups)
    copies[1].wait()
    prob = prob_ref[...].astype(f32)
    prob_at = jnp.where(hots[0], prob[0:1, :], jnp.where(hots[1], prob[1:2, :], 0.0))
    copies[2].wait()
    copies[3].wait()
    for r in range(CAP):
        x = mul(picks[r].astype(bf16), tok_ref[...], NN)
        q = mul((picks[r] * prob_at).astype(bf16), cot_ref[...], NN)
        for c in range(chunks):
            cols = slice(c * LANES, (c + 1) * LANES)
            stage[pl.ds(c, groups, stride=sub), :] = x[:, cols]
            stage[pl.ds(chunks + c, groups, stride=sub), :] = q[:, cols]
        out_ref[:, r] = stage[...].reshape(groups, sub, LANES).astype(bf16)


def dispatch(ids_t, prob_t, tokens, cotangent, groups):
    sub = 2 * tokens.shape[1] // LANES
    return call(
        dispatch_body,
        jax.ShapeDtypeStruct((groups, CAP, sub, LANES), bf16),
        [pltpu.VMEM(a.shape, a.dtype) for a in (ids_t, prob_t, tokens, cotangent)]
        + [pltpu.VMEM((groups * sub, LANES), f32), pltpu.SemaphoreType.DMA((4,))],
        2 * 2 * CAP * groups * tokens.size,
        4 * 2**20,
        [pl.BlockSpec(memory_space=pl.ANY)] * 4,
        60,
    )(ids_t, prob_t, tokens, cotangent)


def rows_body(
    place_ref, got_ref, w0_hbm, w1_hbm, w2_hbm, w3_hbm, back_hbm, x_hbm, q_hbm, da_hbm, du_hbm, h_hbm,
    w_ref, back_ref, x_ref, q_ref, da_ref, du_ref, h_ref, stage, stage_back, sems,
):
    depth = w0_hbm.shape[1]
    pairs = [
        (w_hbm, w_ref.at[:, pl.ds(pl.multiple_of(place_ref[i] * depth, depth), depth), :])
        for i, w_hbm in enumerate((w0_hbm, w1_hbm, w2_hbm, w3_hbm))
    ]
    parts = len(pairs)
    pairs += [
        (x_ref, x_hbm),
        (q_ref, q_hbm),
        (h_ref, h_hbm),
        (da_ref, da_hbm),
        (du_ref, du_hbm),
        (back_ref, back_hbm),
    ]
    copies = [pltpu.make_async_copy(src, dst, sems.at[i]) for i, (src, dst) in enumerate(pairs)]
    for copy in copies[:parts]:
        copy.start()
    groups, _, sub, _ = got_ref.shape
    chunks = sub // 2
    for r in range(CAP):
        stage[...] = got_ref[:, r].astype(f32).reshape(groups * sub, LANES)
        at = slice(r * groups, (r + 1) * groups)
        for c in range(chunks):
            cols = slice(c * LANES, (c + 1) * LANES)
            x_ref[at, cols] = stage[pl.ds(c, groups, stride=sub), :].astype(bf16)
            q_ref[at, cols] = stage[pl.ds(chunks + c, groups, stride=sub), :].astype(bf16)
    for copy in copies[:parts]:
        copy.wait()
    for copy in copies[parts : parts + 2]:
        copy.start()
    x = x_ref[...]
    a = mul(x, w_ref[0], NN)
    u = mul(x, w_ref[1], NN)
    dh = mul(q_ref[...], w_ref[2], NN)
    sig = jax.nn.sigmoid(a)
    silu = a * sig
    h = (silu * u).astype(bf16)
    da = (dh * u * (sig * (1.0 + a * (1.0 - sig)))).astype(bf16)
    du = (dh * silu).astype(bf16)
    h_ref[...] = h
    da_ref[...] = da
    du_ref[...] = du
    for copy in copies[parts + 2 : parts + 5]:
        copy.start()
    gate = jnp.sum(h.astype(f32) * dh, axis=1, keepdims=True)
    rows = mul(da, w_ref[0], NT) + mul(du, w_ref[1], NT)
    lines = stage_back.shape[0] // groups
    lane = lax.broadcasted_iota(jnp.int32, (groups, LANES), 1)
    gates = jnp.zeros((groups, LANES), f32)
    for r in range(CAP):
        at = slice(r * groups, (r + 1) * groups)
        for c in range(chunks):
            stage_back[pl.ds(r * chunks + c, groups, stride=lines), :] = rows[at, c * LANES : (c + 1) * LANES]
        gates = jnp.where(lane == r, gate[at], gates)
    stage_back[pl.ds(CAP * chunks, groups, stride=lines), :] = gates
    for spare in range(CAP * chunks + 1, lines):
        stage_back[pl.ds(spare, groups, stride=lines), :] = jnp.zeros((groups, LANES), f32)
    back_ref[...] = stage_back[...].reshape(back_ref.shape).astype(bf16)
    copies[parts + 5].start()
    for copy in copies[parts:]:
        copy.wait()


def rows_step(place, got, pieces):
    groups, _, sub, _ = got.shape
    three, depth, hidden = pieces[0].shape
    width = depth * len(pieces)
    rows, chunks = groups * CAP, sub // 2
    lines = -(-(CAP * chunks + 1) // 2) * 2
    made = [(groups * lines // 8, 8, LANES)] + [(rows, width)] * 2 + [(rows, hidden)] * 3
    anywhere = pl.BlockSpec(memory_space=pl.ANY)
    return pl.pallas_call(
        rows_body,
        out_shape=[jax.ShapeDtypeStruct(s, bf16) for s in made],
        in_specs=[pl.BlockSpec(memory_space=pltpu.SMEM), pl.BlockSpec(memory_space=pltpu.VMEM)]
        + [anywhere] * len(pieces),
        out_specs=[anywhere] * len(made),
        scratch_shapes=[pltpu.VMEM(s, bf16) for s in [(three, width, hidden)] + made]
        + [pltpu.VMEM((groups * sub, LANES), f32), pltpu.VMEM((groups * lines, LANES), f32)]
        + [pltpu.SemaphoreType.DMA((len(pieces) + len(made),))],
        compiler_params=pltpu.CompilerParams(vmem_limit_bytes=55 * 2**20),
        cost_estimate=pl.CostEstimate(
            flops=10 * rows * width * hidden, bytes_accessed=8 * 2**20, transcendentals=0
        ),
    )(place, got, *pieces)


def grads_body(core_ref, x_ref, q_ref, da_ref, du_ref, h_ref, keep_ref, send_ref):
    halves, _, depth, _ = keep_ref.shape
    for out_ref, core in ((send_ref, 1 - core_ref[0]), (keep_ref, core_ref[0])):
        for half in range(halves):
            cols = pl.ds(pl.multiple_of((half * 2 + core) * depth, depth), depth)
            out_ref[half, 0] = mul(x_ref[:, cols], da_ref[...], TN).astype(bf16)
            out_ref[half, 1] = mul(x_ref[:, cols], du_ref[...], TN).astype(bf16)
            out_ref[half, 2] = mul(q_ref[:, cols], h_ref[...], TN).astype(bf16)


def weight_grads(core, x, q, da, du, h):
    rows, width = x.shape
    hidden = h.shape[1]
    vmem = pl.BlockSpec(memory_space=pltpu.VMEM)
    half = jax.ShapeDtypeStruct((2, 3, width // 4, hidden), bf16)
    return call(
        grads_body,
        (half, half),
        [],
        6 * rows * width * hidden,
        6 * 2**20,
        [pl.BlockSpec(memory_space=pltpu.SMEM)] + [vmem] * 5,
    )(core, x, q, da, du, h)


def pair_body(side_ref, keep_ref, got_ref, own_ref, send_ref):
    side = side_ref[0]
    send_ref[...] = (keep_ref[1 - side].astype(f32) + got_ref[1 - side].astype(f32)).astype(bf16)
    own_ref[...] = keep_ref[side].astype(f32) + got_ref[side].astype(f32)


def pair_sum(side, keep, got):
    vmem = pl.BlockSpec(memory_space=pltpu.VMEM)
    return pl.pallas_call(
        pair_body,
        out_shape=(
            jax.ShapeDtypeStruct(keep.shape[1:], f32),
            jax.ShapeDtypeStruct(keep.shape[1:], bf16),
        ),
        in_specs=[pl.BlockSpec(memory_space=pltpu.SMEM), vmem, vmem],
        out_specs=(vmem, vmem),
        compiler_params=pltpu.CompilerParams(vmem_limit_bytes=16 * 2**20),
        cost_estimate=pl.CostEstimate(flops=keep.size, bytes_accessed=5 * keep.size, transcendentals=0),
    )(side, keep, got)


def adam_body(own_ref, other_ref, one_ref, two_ref, out_ref, stage):
    blocks = own_ref.shape[1] // LANES
    lines = own_ref.shape[0] * blocks // SLOTS
    for p in range(lines // blocks):
        at = slice(p * SLOTS, (p + 1) * SLOTS)
        grad = own_ref[at, :] + other_ref[at, :].astype(f32)
        first_new = BETA_ONE * one_ref[at, :] + (1.0 - BETA_ONE) * grad
        second_new = BETA_TWO * two_ref[at, :] + (1.0 - BETA_TWO) * grad * grad
        first_hat = first_new * (1.0 / (1.0 - BETA_ONE**STEP))
        second_hat = second_new * (1.0 / (1.0 - BETA_TWO**STEP))
        update = first_hat / (jnp.sqrt(second_hat) + ADAM_EPS)
        for b in range(blocks):
            stage[pl.ds(p * blocks + b, SLOTS, stride=lines), :] = update[:, b * LANES : (b + 1) * LANES]
    out_ref[...] = stage[...].reshape(out_ref.shape).astype(bf16)


def adam_update(own, other, moment_one, moment_two):
    return call(
        adam_body,
        jax.ShapeDtypeStruct((own.size // (8 * LANES), 8, LANES), bf16),
        [pltpu.VMEM((own.size // LANES, LANES), f32)],
        12 * own.size,
        14 * own.size,
    )(own, other, moment_one, moment_two)


def swap_body(partner_ref, in_ref, out_ref):
    def step(d, carry):
        out_ref[d] = in_ref[partner_ref[d]]
        return carry

    lax.fori_loop(0, in_ref.shape[0], step, 0, unroll=8)


def swap_slots(partner, spread):
    vmem = pl.BlockSpec(memory_space=pltpu.VMEM)
    return call(
        swap_body,
        jax.ShapeDtypeStruct(spread.shape, spread.dtype),
        [],
        0,
        4 * spread.size,
        [pl.BlockSpec(memory_space=pltpu.SMEM), vmem],
    )(partner, spread)


def collect_body(in_ref, out_ref, stage):
    stage[...] = in_ref[...].astype(f32).reshape(stage.shape)
    blocks = out_ref.shape[1] // LANES
    lines = stage.shape[0] // SLOTS
    for p in range(lines // blocks):
        for b in range(blocks):
            out_ref[p * SLOTS : (p + 1) * SLOTS, b * LANES : (b + 1) * LANES] = stage[
                pl.ds(p * blocks + b, SLOTS, stride=lines), :
            ].astype(bf16)


def collect(routed, shape):
    return call(
        collect_body,
        jax.ShapeDtypeStruct(shape, bf16),
        [pltpu.VMEM((routed.size // LANES, LANES), f32)],
        0,
        4 * routed.size,
    )(routed)


def combine_body(ids_ref, prob_ref, back_ref, tok_ref, gate_ref, stage, rows):
    groups, chunks = rows.shape[0] // CAP, rows.shape[1] // LANES
    lines = stage.shape[0] // groups
    hots, picks = routing(ids_ref[...], groups)
    stage[...] = back_ref[...].astype(f32).reshape(stage.shape)
    for r in range(CAP):
        for c in range(chunks):
            rows[r * groups : (r + 1) * groups, c * LANES : (c + 1) * LANES] = stage[
                pl.ds(r * chunks + c, groups, stride=lines), :
            ].astype(bf16)
    tok_ref[...] = mul(jnp.concatenate(picks, axis=0).astype(bf16), rows[...], TN).astype(bf16)
    gates = stage[pl.ds(CAP * chunks, groups, stride=lines), :]
    gate_at = sum(picks[r] * gates[:, r : r + 1] for r in range(CAP))
    for k in range(2):
        total = jnp.sum(jnp.where(hots[k], gate_at, 0.0), axis=0, keepdims=True)
        gate_ref[k : k + 1, :] = total / prob_ref[k : k + 1, :].astype(f32)


def combine(ids_t, prob_t, back, width, groups):
    tok_count = ids_t.shape[1]
    return call(
        combine_body,
        (
            jax.ShapeDtypeStruct((tok_count, width), bf16),
            jax.ShapeDtypeStruct((2, tok_count), f32),
        ),
        [
            pltpu.VMEM((back.size // LANES, LANES), f32),
            pltpu.VMEM((groups * CAP, width), bf16),
        ],
        2 * CAP * groups * tok_count * width,
        4 * 2**20,
    )(ids_t, prob_t, back)


def on_device(
    tokens,
    cotangent,
    route_ids,
    gate_prob,
    swap_partner,
    expert_weights,
    first_moment,
    second_moment,
):
    groups = lax.axis_size("expert")
    hidden = expert_weights.shape[3]
    flat = (expert_weights.size // hidden, hidden)
    ids_t, prob_t = route_ids.T, gate_prob.T
    replica = lax.axis_index("dp")
    core, side = (replica % 2).reshape(1), (replica // 2).reshape(1)
    tiles, pairs = (-1, 8, LANES), (groups, -1, 2, LANES)

    sent = dispatch(ids_t, prob_t, tokens, cotangent, groups)
    mine, sent = lax.optimization_barrier((expert_weights[0], sent))
    got = exchange(sent)
    far = lax.ppermute(mine, "dp", ACROSS)
    pieces = (mine, far, lax.ppermute(mine, "dp", BESIDE), lax.ppermute(far, "dp", BESIDE))
    near = side * 2
    place = jnp.concatenate([near + core, 2 - near + core, near + 1 - core, 3 - near - core])
    returned, *operands = rows_step(place, got, pieces)
    keep, sent = weight_grads(core, *operands)
    own, sent = pair_sum(side, keep, lax.ppermute(sent, "dp", BESIDE))
    back = exchange(returned.reshape(pairs))
    other = lax.ppermute(sent, "dp", ACROSS)
    staged = adam_update(
        own.reshape(flat), other.reshape(flat), first_moment.reshape(flat), second_moment.reshape(flat)
    )
    back, staged = lax.optimization_barrier((back, staged))
    spread = exchange(staged.reshape(pairs))
    routed = exchange(swap_slots(swap_partner, spread))
    token_grad, gate_grad = combine(ids_t, prob_t, back.reshape(tiles), tokens.shape[1], groups)
    update = collect(routed.reshape(tiles), flat)
    return (token_grad, gate_grad.T.astype(bf16), update.reshape(expert_weights.shape))


def solution(mesh):
    placed = (
        P(("expert", "dp"), None),
        P(("expert", "dp"), None),
        P(("expert", "dp"), None),
        P(("expert", "dp"), None),
        P(),
        P("expert", None, "dp", None),
        P("expert", None, "dp", None),
        P("expert", None, "dp", None),
    )
    return jax.shard_map(
        on_device,
        mesh=mesh,
        in_specs=placed,
        out_specs=(
            P(("expert", "dp"), None),
            P(("expert", "dp"), None),
            P("expert", None, "dp", None),
        ),
        check_vma=False,
    )
```

```python
import jax
import jax.numpy as jnp
from jax import lax
from jax.experimental import pallas as pl
from jax.experimental.pallas import tpu as pltpu
from jax.sharding import PartitionSpec as P

STEP = 100
BETA_ONE = 0.9
BETA_TWO = 0.95
ADAM_EPS = 1e-08
CAP = 3
LANES = 128
SLOTS = 128
BESIDE = [(0, 1), (1, 0), (2, 3), (3, 2)]
ACROSS = [(0, 2), (2, 0), (1, 3), (3, 1)]
f32, bf16 = jnp.float32, jnp.bfloat16

NN = (((1,), (0,)), ((), ()))
NT = (((1,), (1,)), ((), ()))
TN = (((0,), (0,)), ((), ()))


def mul(a, b, dims):
    return lax.dot_general(a, b, dims, preferred_element_type=f32)


def call(body, outs, scratch, flops, moved, ins=None, limit=16, out=None):
    return pl.pallas_call(
        body,
        out_shape=outs,
        **({} if ins is None else {"in_specs": ins}),
        **({} if out is None else {"out_specs": out}),
        scratch_shapes=scratch,
        compiler_params=pltpu.CompilerParams(vmem_limit_bytes=limit * 2**20),
        cost_estimate=pl.CostEstimate(flops=flops, bytes_accessed=moved, transcendentals=0),
    )


def exchange(x):
    return lax.all_to_all(x, "expert", split_axis=0, concat_axis=0, tiled=True)


def routing(ids, groups):
    tok_count = ids.shape[1]
    expert = lax.broadcasted_iota(jnp.int32, (groups, tok_count), 0)
    hots = [ids[k : k + 1, :] == expert for k in range(2)]
    named = jnp.where(hots[0] | hots[1], 1.0, 0.0)
    before = lax.broadcasted_iota(jnp.int32, (tok_count, tok_count), 0)
    after = lax.broadcasted_iota(jnp.int32, (tok_count, tok_count), 1)
    earlier = jnp.where(before < after, 1.0, 0.0).astype(bf16)
    rank = mul(named.astype(bf16), earlier, NN)
    return hots, [jnp.where(rank == r, named, 0.0) for r in range(CAP)]


def dispatch_body(
    ids_hbm, prob_hbm, tok_hbm, cot_hbm, out_hbm, ids_ref, prob_ref, tok_ref, cot_ref, out_ref, stage, sems
):
    pairs = ((ids_hbm, ids_ref), (prob_hbm, prob_ref), (tok_hbm, tok_ref), (cot_hbm, cot_ref))
    copies = [pltpu.make_async_copy(src, dst, sems.at[i]) for i, (src, dst) in enumerate(pairs)]
    for copy in copies:
        copy.start()
    leaving = [
        pltpu.make_async_copy(out_ref.at[r], out_hbm.at[:, r], sems.at[len(pairs) + r]) for r in range(CAP)
    ]
    _, groups, sub, _ = out_ref.shape
    chunks = sub // 2
    copies[0].wait()
    hots, picks = routing(ids_ref[...], groups)
    copies[1].wait()
    prob = prob_ref[...].astype(f32)
    prob_at = jnp.where(hots[0], prob[0:1, :], jnp.where(hots[1], prob[1:2, :], 0.0))
    copies[2].wait()
    for r in range(CAP):
        x = mul(picks[r].astype(bf16), tok_ref[...], NN)
        for c in range(chunks):
            stage[r, pl.ds(c, groups, stride=sub), :] = x[:, c * LANES : (c + 1) * LANES]
    copies[3].wait()
    for r in range(CAP):
        q = mul((picks[r] * prob_at).astype(bf16), cot_ref[...], NN)
        for c in range(chunks):
            stage[r, pl.ds(chunks + c, groups, stride=sub), :] = q[:, c * LANES : (c + 1) * LANES]
        out_ref[r] = stage[r].reshape(groups, sub, LANES).astype(bf16)
        leaving[r].start()
    for copy in leaving:
        copy.wait()


def dispatch(ids_t, prob_t, tokens, cotangent, groups):
    sub = 2 * tokens.shape[1] // LANES
    arrays = (ids_t, prob_t, tokens, cotangent)
    return call(
        dispatch_body,
        pltpu.HBM((groups, CAP, sub, LANES), bf16),
        [pltpu.VMEM(a.shape, a.dtype) for a in arrays]
        + [pltpu.VMEM((CAP, groups, sub, LANES), bf16), pltpu.VMEM((CAP, groups * sub, LANES), f32)]
        + [pltpu.SemaphoreType.DMA((len(arrays) + CAP,))],
        2 * 2 * CAP * groups * tokens.size,
        4 * 2**20,
        [pl.BlockSpec(memory_space=pl.ANY)] * len(arrays),
        60,
        pl.BlockSpec(memory_space=pl.ANY),
    )(*arrays)


def rows_body(
    place_ref, got_ref, w0_hbm, w1_hbm, w2_hbm, w3_hbm, back_hbm, x_hbm, q_hbm, da_hbm, du_hbm, h_hbm,
    w_ref, back_ref, x_ref, q_ref, da_ref, du_ref, h_ref, stage, stage_back, sems,
):
    depth = w0_hbm.shape[1]
    pairs = [
        (w_hbm, w_ref.at[:, pl.ds(pl.multiple_of(place_ref[i] * depth, depth), depth), :])
        for i, w_hbm in enumerate((w0_hbm, w1_hbm, w2_hbm, w3_hbm))
    ]
    parts = len(pairs)
    pairs += [
        (x_ref, x_hbm),
        (q_ref, q_hbm),
        (h_ref, h_hbm),
        (da_ref, da_hbm),
        (du_ref, du_hbm),
        (back_ref, back_hbm),
    ]
    copies = [pltpu.make_async_copy(src, dst, sems.at[i]) for i, (src, dst) in enumerate(pairs)]
    for copy in copies[:parts]:
        copy.start()
    groups, _, sub, _ = got_ref.shape
    chunks = sub // 2
    for r in range(CAP):
        stage[...] = got_ref[:, r].astype(f32).reshape(groups * sub, LANES)
        at = slice(r * groups, (r + 1) * groups)
        for c in range(chunks):
            cols = slice(c * LANES, (c + 1) * LANES)
            x_ref[at, cols] = stage[pl.ds(c, groups, stride=sub), :].astype(bf16)
            q_ref[at, cols] = stage[pl.ds(chunks + c, groups, stride=sub), :].astype(bf16)
    for copy in copies[:parts]:
        copy.wait()
    for copy in copies[parts : parts + 2]:
        copy.start()
    x = x_ref[...]
    a = mul(x, w_ref[0], NN)
    u = mul(x, w_ref[1], NN)
    dh = mul(q_ref[...], w_ref[2], NN)
    sig = jax.nn.sigmoid(a)
    silu = a * sig
    h = (silu * u).astype(bf16)
    da = (dh * u * (sig * (1.0 + a * (1.0 - sig)))).astype(bf16)
    du = (dh * silu).astype(bf16)
    h_ref[...] = h
    da_ref[...] = da
    du_ref[...] = du
    for copy in copies[parts + 2 : parts + 5]:
        copy.start()
    gate = jnp.sum(h.astype(f32) * dh, axis=1, keepdims=True)
    rows = mul(da, w_ref[0], NT) + mul(du, w_ref[1], NT)
    lines = stage_back.shape[0] // groups
    lane = lax.broadcasted_iota(jnp.int32, (groups, LANES), 1)
    gates = jnp.zeros((groups, LANES), f32)
    for r in range(CAP):
        at = slice(r * groups, (r + 1) * groups)
        for c in range(chunks):
            stage_back[pl.ds(r * chunks + c, groups, stride=lines), :] = rows[at, c * LANES : (c + 1) * LANES]
        gates = jnp.where(lane == r, gate[at], gates)
    stage_back[pl.ds(CAP * chunks, groups, stride=lines), :] = gates
    for spare in range(CAP * chunks + 1, lines):
        stage_back[pl.ds(spare, groups, stride=lines), :] = jnp.zeros((groups, LANES), f32)
    back_ref[...] = stage_back[...].reshape(back_ref.shape).astype(bf16)
    copies[parts + 5].start()
    for copy in copies[parts:]:
        copy.wait()


def rows_step(place, got, pieces):
    groups, _, sub, _ = got.shape
    three, depth, hidden = pieces[0].shape
    width = depth * len(pieces)
    rows, chunks = groups * CAP, sub // 2
    lines = -(-(CAP * chunks + 1) // 2) * 2
    made = [(groups * lines // 8, 8, LANES)] + [(rows, width)] * 2 + [(rows, hidden)] * 3
    anywhere = pl.BlockSpec(memory_space=pl.ANY)
    return pl.pallas_call(
        rows_body,
        out_shape=[pltpu.HBM(s, bf16) for s in made],
        in_specs=[pl.BlockSpec(memory_space=pltpu.SMEM), pl.BlockSpec(memory_space=pltpu.VMEM)]
        + [anywhere] * len(pieces),
        out_specs=[anywhere] * len(made),
        scratch_shapes=[pltpu.VMEM(s, bf16) for s in [(three, width, hidden)] + made]
        + [pltpu.VMEM((groups * sub, LANES), f32), pltpu.VMEM((groups * lines, LANES), f32)]
        + [pltpu.SemaphoreType.DMA((len(pieces) + len(made),))],
        compiler_params=pltpu.CompilerParams(vmem_limit_bytes=44 * 2**20),
        cost_estimate=pl.CostEstimate(
            flops=10 * rows * width * hidden, bytes_accessed=8 * 2**20, transcendentals=0
        ),
    )(place, got, *pieces)


def grads_body(core_ref, x_ref, q_ref, da_ref, du_ref, h_ref, keep_ref, send_ref):
    halves, _, depth, _ = keep_ref.shape
    for out_ref, core in ((send_ref, 1 - core_ref[0]), (keep_ref, core_ref[0])):
        for half in range(halves):
            cols = pl.ds(pl.multiple_of((half * 2 + core) * depth, depth), depth)
            out_ref[half, 0] = mul(x_ref[:, cols], da_ref[...], TN).astype(bf16)
            out_ref[half, 1] = mul(x_ref[:, cols], du_ref[...], TN).astype(bf16)
            out_ref[half, 2] = mul(q_ref[:, cols], h_ref[...], TN).astype(bf16)


def weight_grads(core, x, q, da, du, h):
    rows, width = x.shape
    hidden = h.shape[1]
    vmem = pl.BlockSpec(memory_space=pltpu.VMEM)
    half = jax.ShapeDtypeStruct((2, 3, width // 4, hidden), bf16)
    return call(
        grads_body,
        (half, half),
        [],
        6 * rows * width * hidden,
        6 * 2**20,
        [pl.BlockSpec(memory_space=pltpu.SMEM)] + [vmem] * 5,
    )(core, x, q, da, du, h)


def pair_body(side_ref, keep_ref, got_ref, own_ref, send_ref):
    side = side_ref[0]
    send_ref[...] = (keep_ref[1 - side].astype(f32) + got_ref[1 - side].astype(f32)).astype(bf16)
    own_ref[...] = keep_ref[side].astype(f32) + got_ref[side].astype(f32)


def pair_sum(side, keep, got):
    vmem = pl.BlockSpec(memory_space=pltpu.VMEM)
    return pl.pallas_call(
        pair_body,
        out_shape=(
            jax.ShapeDtypeStruct(keep.shape[1:], f32),
            jax.ShapeDtypeStruct(keep.shape[1:], bf16),
        ),
        in_specs=[pl.BlockSpec(memory_space=pltpu.SMEM), vmem, vmem],
        out_specs=(vmem, vmem),
        compiler_params=pltpu.CompilerParams(vmem_limit_bytes=16 * 2**20),
        cost_estimate=pl.CostEstimate(flops=keep.size, bytes_accessed=5 * keep.size, transcendentals=0),
    )(side, keep, got)


def adam_body(own_ref, other_ref, one_ref, two_ref, out_ref, stage):
    blocks = own_ref.shape[1] // LANES
    lines = own_ref.shape[0] * blocks // SLOTS
    for p in range(lines // blocks):
        at = slice(p * SLOTS, (p + 1) * SLOTS)
        grad = own_ref[at, :] + other_ref[at, :].astype(f32)
        first_new = BETA_ONE * one_ref[at, :] + (1.0 - BETA_ONE) * grad
        second_new = BETA_TWO * two_ref[at, :] + (1.0 - BETA_TWO) * grad * grad
        first_hat = first_new * (1.0 / (1.0 - BETA_ONE**STEP))
        second_hat = second_new * (1.0 / (1.0 - BETA_TWO**STEP))
        update = first_hat / (jnp.sqrt(second_hat) + ADAM_EPS)
        for b in range(blocks):
            stage[pl.ds(p * blocks + b, SLOTS, stride=lines), :] = update[:, b * LANES : (b + 1) * LANES]
    out_ref[...] = stage[...].reshape(out_ref.shape).astype(bf16)


def adam_update(own, other, moment_one, moment_two):
    return call(
        adam_body,
        jax.ShapeDtypeStruct((own.size // (8 * LANES), 8, LANES), bf16),
        [pltpu.VMEM((own.size // LANES, LANES), f32)],
        12 * own.size,
        14 * own.size,
    )(own, other, moment_one, moment_two)


def swap_body(partner_ref, in_ref, out_ref):
    def step(d, carry):
        out_ref[d] = in_ref[partner_ref[d]]
        return carry

    lax.fori_loop(0, in_ref.shape[0], step, 0, unroll=8)


def swap_slots(partner, spread):
    vmem = pl.BlockSpec(memory_space=pltpu.VMEM)
    return call(
        swap_body,
        jax.ShapeDtypeStruct(spread.shape, spread.dtype),
        [],
        0,
        4 * spread.size,
        [pl.BlockSpec(memory_space=pltpu.SMEM), vmem],
    )(partner, spread)


def collect_body(in_ref, out_ref, stage):
    stage[...] = in_ref[...].astype(f32).reshape(stage.shape)
    blocks = out_ref.shape[1] // LANES
    lines = stage.shape[0] // SLOTS
    for p in range(lines // blocks):
        for b in range(blocks):
            out_ref[p * SLOTS : (p + 1) * SLOTS, b * LANES : (b + 1) * LANES] = stage[
                pl.ds(p * blocks + b, SLOTS, stride=lines), :
            ].astype(bf16)


def collect(routed, shape):
    return call(
        collect_body,
        jax.ShapeDtypeStruct(shape, bf16),
        [pltpu.VMEM((routed.size // LANES, LANES), f32)],
        0,
        4 * routed.size,
    )(routed)


def combine_body(ids_ref, prob_ref, back_ref, tok_ref, gate_ref, stage, rows):
    groups, chunks = rows.shape[0] // CAP, rows.shape[1] // LANES
    lines = stage.shape[0] // groups
    hots, picks = routing(ids_ref[...], groups)
    stage[...] = back_ref[...].astype(f32).reshape(stage.shape)
    for r in range(CAP):
        for c in range(chunks):
            rows[r * groups : (r + 1) * groups, c * LANES : (c + 1) * LANES] = stage[
                pl.ds(r * chunks + c, groups, stride=lines), :
            ].astype(bf16)
    tok_ref[...] = mul(jnp.concatenate(picks, axis=0).astype(bf16), rows[...], TN).astype(bf16)
    gates = stage[pl.ds(CAP * chunks, groups, stride=lines), :]
    gate_at = sum(picks[r] * gates[:, r : r + 1] for r in range(CAP))
    for k in range(2):
        total = jnp.sum(jnp.where(hots[k], gate_at, 0.0), axis=0, keepdims=True)
        gate_ref[k : k + 1, :] = total / prob_ref[k : k + 1, :].astype(f32)


def combine(ids_t, prob_t, back, width, groups):
    tok_count = ids_t.shape[1]
    return call(
        combine_body,
        (
            jax.ShapeDtypeStruct((tok_count, width), bf16),
            jax.ShapeDtypeStruct((2, tok_count), f32),
        ),
        [
            pltpu.VMEM((back.size // LANES, LANES), f32),
            pltpu.VMEM((groups * CAP, width), bf16),
        ],
        2 * CAP * groups * tok_count * width,
        4 * 2**20,
    )(ids_t, prob_t, back)


def on_device(
    tokens,
    cotangent,
    route_ids,
    gate_prob,
    swap_partner,
    expert_weights,
    first_moment,
    second_moment,
):
    groups = lax.axis_size("expert")
    hidden = expert_weights.shape[3]
    flat = (expert_weights.size // hidden, hidden)
    ids_t, prob_t = route_ids.T, gate_prob.T
    replica = lax.axis_index("dp")
    core, side = (replica % 2).reshape(1), (replica // 2).reshape(1)
    tiles, pairs = (-1, 8, LANES), (groups, -1, 2, LANES)

    sent = dispatch(ids_t, prob_t, tokens, cotangent, groups)
    mine, sent = lax.optimization_barrier((expert_weights[0], sent))
    got = exchange(sent)
    far = lax.ppermute(mine, "dp", ACROSS)
    pieces = (mine, far, lax.ppermute(mine, "dp", BESIDE), lax.ppermute(far, "dp", BESIDE))
    near = side * 2
    place = jnp.concatenate([near + core, 2 - near + core, near + 1 - core, 3 - near - core])
    returned, *operands = rows_step(place, got, pieces)
    keep, sent = weight_grads(core, *operands)
    own, sent = pair_sum(side, keep, lax.ppermute(sent, "dp", BESIDE))
    back = exchange(returned.reshape(pairs))
    other = lax.ppermute(sent, "dp", ACROSS)
    staged = adam_update(
        own.reshape(flat), other.reshape(flat), first_moment.reshape(flat), second_moment.reshape(flat)
    )
    back, staged = lax.optimization_barrier((back, staged))
    spread = exchange(staged.reshape(pairs))
    routed = exchange(swap_slots(swap_partner, spread))
    token_grad, gate_grad = combine(ids_t, prob_t, back.reshape(tiles), tokens.shape[1], groups)
    update = collect(routed.reshape(tiles), flat)
    return (token_grad, gate_grad.T.astype(bf16), update.reshape(expert_weights.shape))


def solution(mesh):
    placed = (
        P(("expert", "dp"), None),
        P(("expert", "dp"), None),
        P(("expert", "dp"), None),
        P(("expert", "dp"), None),
        P(),
        P("expert", None, "dp", None),
        P("expert", None, "dp", None),
        P("expert", None, "dp", None),
    )
    return jax.shard_map(
        on_device,
        mesh=mesh,
        in_specs=placed,
        out_specs=(
            P(("expert", "dp"), None),
            P(("expert", "dp"), None),
            P("expert", None, "dp", None),
        ),
        check_vma=False,
    )
```

```python
import jax
import jax.numpy as jnp
from jax import lax
from jax.experimental import pallas as pl
from jax.experimental.pallas import tpu as pltpu
from jax.sharding import PartitionSpec as P

STEP = 100
BETA_ONE = 0.9
BETA_TWO = 0.95
ADAM_EPS = 1e-08
CAP = 3
LANES = 128
BESIDE = [(0, 1), (1, 0), (2, 3), (3, 2)]
ACROSS = [(0, 2), (2, 0), (1, 3), (3, 1)]
f32, bf16 = jnp.float32, jnp.bfloat16

NN = (((1,), (0,)), ((), ()))
NT = (((1,), (1,)), ((), ()))
TN = (((0,), (0,)), ((), ()))


def mul(a, b, dims):
    return lax.dot_general(a, b, dims, preferred_element_type=f32)


def call(body, outs, scratch, flops, moved, ins=None, limit=16, out=None):
    return pl.pallas_call(
        body,
        out_shape=outs,
        **({} if ins is None else {"in_specs": ins}),
        **({} if out is None else {"out_specs": out}),
        scratch_shapes=scratch,
        compiler_params=pltpu.CompilerParams(vmem_limit_bytes=limit * 2**20),
        cost_estimate=pl.CostEstimate(flops=flops, bytes_accessed=moved, transcendentals=0),
    )


def exchange(x):
    return lax.all_to_all(x, "expert", split_axis=0, concat_axis=0, tiled=True)


def routing(ids, groups):
    tok_count = ids.shape[1]
    expert = lax.broadcasted_iota(jnp.int32, (groups, tok_count), 0)
    hots = [ids[k : k + 1, :] == expert for k in range(2)]
    named = jnp.where(hots[0] | hots[1], 1.0, 0.0)
    before = lax.broadcasted_iota(jnp.int32, (tok_count, tok_count), 0)
    after = lax.broadcasted_iota(jnp.int32, (tok_count, tok_count), 1)
    earlier = jnp.where(before < after, 1.0, 0.0).astype(bf16)
    rank = mul(named.astype(bf16), earlier, NN)
    return hots, [jnp.where(rank == r, named, 0.0) for r in range(CAP)]


def dispatch_body(
    ids_hbm, prob_hbm, tok_hbm, cot_hbm, out_hbm, ids_ref, prob_ref, tok_ref, cot_ref, out_ref, stage, sems
):
    pairs = ((ids_hbm, ids_ref), (prob_hbm, prob_ref), (tok_hbm, tok_ref), (cot_hbm, cot_ref))
    copies = [pltpu.make_async_copy(src, dst, sems.at[i]) for i, (src, dst) in enumerate(pairs)]
    for copy in copies:
        copy.start()
    leaving = [
        pltpu.make_async_copy(out_ref.at[r], out_hbm.at[:, r], sems.at[len(pairs) + r]) for r in range(CAP)
    ]
    _, groups, sub, _ = out_ref.shape
    chunks = sub // 2
    copies[0].wait()
    hots, picks = routing(ids_ref[...], groups)
    copies[1].wait()
    prob = prob_ref[...].astype(f32)
    prob_at = jnp.where(hots[0], prob[0:1, :], jnp.where(hots[1], prob[1:2, :], 0.0))
    copies[2].wait()
    for r in range(CAP):
        x = mul(picks[r].astype(bf16), tok_ref[...], NN)
        for c in range(chunks):
            stage[r, pl.ds(c, groups, stride=sub), :] = x[:, c * LANES : (c + 1) * LANES]
    copies[3].wait()
    for r in range(CAP):
        q = mul((picks[r] * prob_at).astype(bf16), cot_ref[...], NN)
        for c in range(chunks):
            stage[r, pl.ds(chunks + c, groups, stride=sub), :] = q[:, c * LANES : (c + 1) * LANES]
        out_ref[r] = stage[r].reshape(groups, sub, LANES).astype(bf16)
        leaving[r].start()
    for copy in leaving:
        copy.wait()


def dispatch(ids_t, prob_t, tokens, cotangent, groups):
    sub = 2 * tokens.shape[1] // LANES
    arrays = (ids_t, prob_t, tokens, cotangent)
    return call(
        dispatch_body,
        pltpu.HBM((groups, CAP, sub, LANES), bf16),
        [pltpu.VMEM(a.shape, a.dtype) for a in arrays]
        + [pltpu.VMEM((CAP, groups, sub, LANES), bf16), pltpu.VMEM((CAP, groups * sub, LANES), f32)]
        + [pltpu.SemaphoreType.DMA((len(arrays) + CAP,))],
        2 * 2 * CAP * groups * tokens.size,
        4 * 2**20,
        [pl.BlockSpec(memory_space=pl.ANY)] * len(arrays),
        60,
        pl.BlockSpec(memory_space=pl.ANY),
    )(*arrays)


def rows_body(
    place_ref, got_ref, w0_hbm, w1_hbm, w2_hbm, w3_hbm, back_hbm, x_hbm, q_hbm, da_hbm, du_hbm, h_hbm,
    w_ref, back_ref, x_ref, q_ref, da_ref, du_ref, h_ref, stage, stage_back, sems,
):
    depth = w0_hbm.shape[1]
    pairs = [
        (w_hbm, w_ref.at[:, pl.ds(pl.multiple_of(place_ref[i] * depth, depth), depth), :])
        for i, w_hbm in enumerate((w0_hbm, w1_hbm, w2_hbm, w3_hbm))
    ]
    parts = len(pairs)
    pairs += [
        (x_ref, x_hbm),
        (q_ref, q_hbm),
        (h_ref, h_hbm),
        (da_ref, da_hbm),
        (du_ref, du_hbm),
        (back_ref, back_hbm),
    ]
    copies = [pltpu.make_async_copy(src, dst, sems.at[i]) for i, (src, dst) in enumerate(pairs)]
    for copy in copies[:parts]:
        copy.start()
    groups, _, sub, _ = got_ref.shape
    chunks = sub // 2
    for r in range(CAP):
        stage[...] = got_ref[:, r].astype(f32).reshape(groups * sub, LANES)
        at = slice(r * groups, (r + 1) * groups)
        for c in range(chunks):
            cols = slice(c * LANES, (c + 1) * LANES)
            x_ref[at, cols] = stage[pl.ds(c, groups, stride=sub), :].astype(bf16)
            q_ref[at, cols] = stage[pl.ds(chunks + c, groups, stride=sub), :].astype(bf16)
    for copy in copies[:parts]:
        copy.wait()
    for copy in copies[parts : parts + 2]:
        copy.start()
    x = x_ref[...]
    a = mul(x, w_ref[0], NN)
    u = mul(x, w_ref[1], NN)
    dh = mul(q_ref[...], w_ref[2], NN)
    sig = jax.nn.sigmoid(a)
    silu = a * sig
    h = (silu * u).astype(bf16)
    da = (dh * u * (sig * (1.0 + a * (1.0 - sig)))).astype(bf16)
    du = (dh * silu).astype(bf16)
    h_ref[...] = h
    da_ref[...] = da
    du_ref[...] = du
    for copy in copies[parts + 2 : parts + 5]:
        copy.start()
    gate = jnp.sum(h.astype(f32) * dh, axis=1, keepdims=True)
    rows = mul(da, w_ref[0], NT) + mul(du, w_ref[1], NT)
    lines = stage_back.shape[0] // groups
    lane = lax.broadcasted_iota(jnp.int32, (groups, LANES), 1)
    gates = jnp.zeros((groups, LANES), f32)
    for r in range(CAP):
        at = slice(r * groups, (r + 1) * groups)
        for c in range(chunks):
            stage_back[pl.ds(r * chunks + c, groups, stride=lines), :] = rows[at, c * LANES : (c + 1) * LANES]
        gates = jnp.where(lane == r, gate[at], gates)
    stage_back[pl.ds(CAP * chunks, groups, stride=lines), :] = gates
    for spare in range(CAP * chunks + 1, lines):
        stage_back[pl.ds(spare, groups, stride=lines), :] = jnp.zeros((groups, LANES), f32)
    back_ref[...] = stage_back[...].reshape(back_ref.shape).astype(bf16)
    copies[parts + 5].start()
    for copy in copies[parts:]:
        copy.wait()


def rows_step(place, got, pieces):
    groups, _, sub, _ = got.shape
    three, depth, hidden = pieces[0].shape
    width = depth * len(pieces)
    rows, chunks = groups * CAP, sub // 2
    lines = -(-(CAP * chunks + 1) // 2) * 2
    made = [(groups * lines // 8, 8, LANES)] + [(rows, width)] * 2 + [(rows, hidden)] * 3
    anywhere = pl.BlockSpec(memory_space=pl.ANY)
    return pl.pallas_call(
        rows_body,
        out_shape=[pltpu.HBM(s, bf16) for s in made],
        in_specs=[pl.BlockSpec(memory_space=pltpu.SMEM), pl.BlockSpec(memory_space=pltpu.VMEM)]
        + [anywhere] * len(pieces),
        out_specs=[anywhere] * len(made),
        scratch_shapes=[pltpu.VMEM(s, bf16) for s in [(three, width, hidden)] + made]
        + [pltpu.VMEM((groups * sub, LANES), f32), pltpu.VMEM((groups * lines, LANES), f32)]
        + [pltpu.SemaphoreType.DMA((len(pieces) + len(made),))],
        compiler_params=pltpu.CompilerParams(vmem_limit_bytes=44 * 2**20),
        cost_estimate=pl.CostEstimate(
            flops=10 * rows * width * hidden, bytes_accessed=8 * 2**20, transcendentals=0
        ),
    )(place, got, *pieces)


def grads_body(core_ref, x_ref, q_ref, da_ref, du_ref, h_ref, keep_ref, send_ref):
    halves, _, depth, _ = keep_ref.shape
    for out_ref, core in ((send_ref, 1 - core_ref[0]), (keep_ref, core_ref[0])):
        for half in range(halves):
            cols = pl.ds(pl.multiple_of((half * 2 + core) * depth, depth), depth)
            out_ref[half, 0] = mul(x_ref[:, cols], da_ref[...], TN).astype(bf16)
            out_ref[half, 1] = mul(x_ref[:, cols], du_ref[...], TN).astype(bf16)
            out_ref[half, 2] = mul(q_ref[:, cols], h_ref[...], TN).astype(bf16)


def weight_grads(core, x, q, da, du, h):
    rows, width = x.shape
    hidden = h.shape[1]
    vmem = pl.BlockSpec(memory_space=pltpu.VMEM)
    half = jax.ShapeDtypeStruct((2, 3, width // 4, hidden), bf16)
    return call(
        grads_body,
        (half, half),
        [],
        6 * rows * width * hidden,
        6 * 2**20,
        [pl.BlockSpec(memory_space=pltpu.SMEM)] + [vmem] * 5,
    )(core, x, q, da, du, h)


def pair_body(side_ref, keep_ref, got_ref, own_ref, send_ref):
    side = side_ref[0]
    send_ref[...] = (keep_ref[1 - side].astype(f32) + got_ref[1 - side].astype(f32)).astype(bf16)
    own_ref[...] = keep_ref[side].astype(f32) + got_ref[side].astype(f32)


def pair_sum(side, keep, got):
    vmem = pl.BlockSpec(memory_space=pltpu.VMEM)
    return pl.pallas_call(
        pair_body,
        out_shape=(
            jax.ShapeDtypeStruct(keep.shape[1:], f32),
            jax.ShapeDtypeStruct(keep.shape[1:], bf16),
        ),
        in_specs=[pl.BlockSpec(memory_space=pltpu.SMEM), vmem, vmem],
        out_specs=(vmem, vmem),
        compiler_params=pltpu.CompilerParams(vmem_limit_bytes=16 * 2**20),
        cost_estimate=pl.CostEstimate(flops=keep.size, bytes_accessed=5 * keep.size, transcendentals=0),
    )(side, keep, got)


def adam_body(own_ref, other_ref, one_ref, two_ref, out_ref):
    bands, blocks, sub, _ = out_ref.shape
    step = 16
    for p in range(0, bands, step):
        at = slice(p * sub, (p + step) * sub)
        grad = own_ref[at, :] + other_ref[at, :].astype(f32)
        first_new = BETA_ONE * one_ref[at, :] + (1.0 - BETA_ONE) * grad
        second_new = BETA_TWO * two_ref[at, :] + (1.0 - BETA_TWO) * grad * grad
        first_hat = first_new * (1.0 / (1.0 - BETA_ONE**STEP))
        second_hat = second_new * (1.0 / (1.0 - BETA_TWO**STEP))
        update = first_hat / (jnp.sqrt(second_hat) + ADAM_EPS)
        for b in range(blocks):
            tiles = update[:, b * LANES : (b + 1) * LANES].reshape(step, sub, LANES)
            out_ref[p : p + step, b] = tiles.astype(bf16)


def adam_update(own, other, moment_one, moment_two):
    rows, hidden = own.shape
    return call(
        adam_body,
        jax.ShapeDtypeStruct((rows // 8, hidden // LANES, 8, LANES), bf16),
        [],
        12 * own.size,
        14 * own.size,
    )(own, other, moment_one, moment_two)


def swap_body(partner_ref, in_ref, out_ref):
    def step(d, carry):
        out_ref[d] = in_ref[partner_ref[d]]
        return carry

    lax.fori_loop(0, in_ref.shape[0], step, 0, unroll=8)


def swap_slots(partner, spread):
    vmem = pl.BlockSpec(memory_space=pltpu.VMEM)
    return call(
        swap_body,
        jax.ShapeDtypeStruct(spread.shape, spread.dtype),
        [],
        0,
        4 * spread.size,
        [pl.BlockSpec(memory_space=pltpu.SMEM), vmem],
    )(partner, spread)


def combine_body(ids_ref, prob_ref, back_ref, tok_ref, gate_ref, stage, rows):
    groups, chunks = rows.shape[0] // CAP, rows.shape[1] // LANES
    lines = stage.shape[0] // groups
    hots, picks = routing(ids_ref[...], groups)
    stage[...] = back_ref[...].astype(f32).reshape(stage.shape)
    for r in range(CAP):
        for c in range(chunks):
            rows[r * groups : (r + 1) * groups, c * LANES : (c + 1) * LANES] = stage[
                pl.ds(r * chunks + c, groups, stride=lines), :
            ].astype(bf16)
    tok_ref[...] = mul(jnp.concatenate(picks, axis=0).astype(bf16), rows[...], TN).astype(bf16)
    gates = stage[pl.ds(CAP * chunks, groups, stride=lines), :]
    gate_at = sum(picks[r] * gates[:, r : r + 1] for r in range(CAP))
    for k in range(2):
        total = jnp.sum(jnp.where(hots[k], gate_at, 0.0), axis=0, keepdims=True)
        gate_ref[k : k + 1, :] = total / prob_ref[k : k + 1, :].astype(f32)


def combine(ids_t, prob_t, back, width, groups):
    tok_count = ids_t.shape[1]
    return call(
        combine_body,
        (
            jax.ShapeDtypeStruct((tok_count, width), bf16),
            jax.ShapeDtypeStruct((2, tok_count), f32),
        ),
        [
            pltpu.VMEM((back.size // LANES, LANES), f32),
            pltpu.VMEM((groups * CAP, width), bf16),
        ],
        2 * CAP * groups * tok_count * width,
        4 * 2**20,
    )(ids_t, prob_t, back)


def on_device(
    tokens,
    cotangent,
    route_ids,
    gate_prob,
    swap_partner,
    expert_weights,
    first_moment,
    second_moment,
):
    groups = lax.axis_size("expert")
    hidden = expert_weights.shape[3]
    flat = (expert_weights.size // hidden, hidden)
    ids_t, prob_t = route_ids.T, gate_prob.T
    replica = lax.axis_index("dp")
    core, side = (replica % 2).reshape(1), (replica // 2).reshape(1)
    tiles, pairs = (-1, 8, LANES), (groups, -1, 2, LANES)

    sent = dispatch(ids_t, prob_t, tokens, cotangent, groups)
    mine, sent = lax.optimization_barrier((expert_weights[0], sent))
    got = exchange(sent)
    far = lax.ppermute(mine, "dp", ACROSS)
    pieces = (mine, far, lax.ppermute(mine, "dp", BESIDE), lax.ppermute(far, "dp", BESIDE))
    near = side * 2
    place = jnp.concatenate([near + core, 2 - near + core, near + 1 - core, 3 - near - core])
    returned, *operands = rows_step(place, got, pieces)
    keep, sent = weight_grads(core, *operands)
    own, sent = pair_sum(side, keep, lax.ppermute(sent, "dp", BESIDE))
    back = exchange(returned.reshape(pairs))
    other = lax.ppermute(sent, "dp", ACROSS)
    staged = adam_update(
        own.reshape(flat), other.reshape(flat), first_moment.reshape(flat), second_moment.reshape(flat)
    )
    back, staged = lax.optimization_barrier((back, staged))
    spread = exchange(staged.reshape(pairs))
    routed = exchange(swap_slots(swap_partner, spread))
    token_grad, gate_grad = combine(ids_t, prob_t, back.reshape(tiles), tokens.shape[1], groups)
    update = routed.reshape(staged.shape).transpose(0, 2, 1, 3)
    return (token_grad, gate_grad.T.astype(bf16), update.reshape(expert_weights.shape))


def solution(mesh):
    placed = (
        P(("expert", "dp"), None),
        P(("expert", "dp"), None),
        P(("expert", "dp"), None),
        P(("expert", "dp"), None),
        P(),
        P("expert", None, "dp", None),
        P("expert", None, "dp", None),
        P("expert", None, "dp", None),
    )
    return jax.shard_map(
        on_device,
        mesh=mesh,
        in_specs=placed,
        out_specs=(
            P(("expert", "dp"), None),
            P(("expert", "dp"), None),
            P("expert", None, "dp", None),
        ),
        check_vma=False,
    )
```

```python
import jax
import jax.numpy as jnp
from jax import lax
from jax.experimental import pallas as pl
from jax.experimental.pallas import tpu as pltpu
from jax.sharding import PartitionSpec as P

STEP = 100
BETA_ONE = 0.9
BETA_TWO = 0.95
ADAM_EPS = 1e-08
CAP = 3
LANES = 128
PORTIONS = 4
BESIDE = [(0, 1), (1, 0), (2, 3), (3, 2)]
ACROSS = [(0, 2), (2, 0), (1, 3), (3, 1)]
f32, bf16 = jnp.float32, jnp.bfloat16

NN = (((1,), (0,)), ((), ()))
NT = (((1,), (1,)), ((), ()))
TN = (((0,), (0,)), ((), ()))


def mul(a, b, dims):
    return lax.dot_general(a, b, dims, preferred_element_type=f32)


def call(body, outs, scratch, flops, moved, ins=None, limit=16, out=None):
    return pl.pallas_call(
        body,
        out_shape=outs,
        **({} if ins is None else {"in_specs": ins}),
        **({} if out is None else {"out_specs": out}),
        scratch_shapes=scratch,
        compiler_params=pltpu.CompilerParams(vmem_limit_bytes=limit * 2**20),
        cost_estimate=pl.CostEstimate(flops=flops, bytes_accessed=moved, transcendentals=0),
    )


def exchange(x):
    return lax.all_to_all(x, "expert", split_axis=0, concat_axis=0, tiled=True)


def routing(ids, groups):
    tok_count = ids.shape[1]
    expert = lax.broadcasted_iota(jnp.int32, (groups, tok_count), 0)
    hots = [ids[k : k + 1, :] == expert for k in range(2)]
    named = jnp.where(hots[0] | hots[1], 1.0, 0.0)
    before = lax.broadcasted_iota(jnp.int32, (tok_count, tok_count), 0)
    after = lax.broadcasted_iota(jnp.int32, (tok_count, tok_count), 1)
    earlier = jnp.where(before < after, 1.0, 0.0).astype(bf16)
    rank = mul(named.astype(bf16), earlier, NN)
    return hots, [jnp.where(rank == r, named, 0.0) for r in range(CAP)]


def dispatch_body(
    ids_hbm, prob_hbm, tok_hbm, cot_hbm, out_hbm, ids_ref, prob_ref, tok_ref, cot_ref, out_ref, stage, sems
):
    pairs = ((ids_hbm, ids_ref), (prob_hbm, prob_ref), (tok_hbm, tok_ref), (cot_hbm, cot_ref))
    copies = [pltpu.make_async_copy(src, dst, sems.at[i]) for i, (src, dst) in enumerate(pairs)]
    for copy in copies:
        copy.start()
    leaving = [
        pltpu.make_async_copy(out_ref.at[r], out_hbm.at[:, r], sems.at[len(pairs) + r]) for r in range(CAP)
    ]
    _, groups, sub, _ = out_ref.shape
    chunks = sub // 2
    copies[0].wait()
    hots, picks = routing(ids_ref[...], groups)
    copies[1].wait()
    prob = prob_ref[...].astype(f32)
    prob_at = jnp.where(hots[0], prob[0:1, :], jnp.where(hots[1], prob[1:2, :], 0.0))
    copies[2].wait()
    for r in range(CAP):
        x = mul(picks[r].astype(bf16), tok_ref[...], NN)
        for c in range(chunks):
            stage[r, pl.ds(c, groups, stride=sub), :] = x[:, c * LANES : (c + 1) * LANES]
    copies[3].wait()
    for r in range(CAP):
        q = mul((picks[r] * prob_at).astype(bf16), cot_ref[...], NN)
        for c in range(chunks):
            stage[r, pl.ds(chunks + c, groups, stride=sub), :] = q[:, c * LANES : (c + 1) * LANES]
        out_ref[r] = stage[r].reshape(groups, sub, LANES).astype(bf16)
        leaving[r].start()
    for copy in leaving:
        copy.wait()


def dispatch(ids_t, prob_t, tokens, cotangent, groups):
    sub = 2 * tokens.shape[1] // LANES
    arrays = (ids_t, prob_t, tokens, cotangent)
    return call(
        dispatch_body,
        pltpu.HBM((groups, CAP, sub, LANES), bf16),
        [pltpu.VMEM(a.shape, a.dtype) for a in arrays]
        + [pltpu.VMEM((CAP, groups, sub, LANES), bf16), pltpu.VMEM((CAP, groups * sub, LANES), f32)]
        + [pltpu.SemaphoreType.DMA((len(arrays) + CAP,))],
        2 * 2 * CAP * groups * tokens.size,
        4 * 2**20,
        [pl.BlockSpec(memory_space=pl.ANY)] * len(arrays),
        60,
        pl.BlockSpec(memory_space=pl.ANY),
    )(*arrays)


def rows_body(
    place_ref, got_ref, w0_hbm, w1_hbm, w2_hbm, w3_hbm, back_hbm, x_hbm, q_hbm, da_hbm, du_hbm, h_hbm,
    w_ref, back_ref, x_ref, q_ref, da_ref, du_ref, h_ref, stage, stage_back, sems,
):
    depth = w0_hbm.shape[1]
    pairs = [
        (w_hbm, w_ref.at[:, pl.ds(pl.multiple_of(place_ref[i] * depth, depth), depth), :])
        for i, w_hbm in enumerate((w0_hbm, w1_hbm, w2_hbm, w3_hbm))
    ]
    parts = len(pairs)
    pairs += [
        (x_ref, x_hbm),
        (q_ref, q_hbm),
        (h_ref, h_hbm),
        (da_ref, da_hbm),
        (du_ref, du_hbm),
    ]
    portion = back_ref.shape[0] // PORTIONS
    cuts = [pl.ds(k * portion, portion) for k in range(PORTIONS)]
    pairs += [(back_ref.at[cut], back_hbm.at[cut]) for cut in cuts]
    copies = [pltpu.make_async_copy(src, dst, sems.at[i]) for i, (src, dst) in enumerate(pairs)]
    for copy in copies[:parts]:
        copy.start()
    groups, _, sub, _ = got_ref.shape
    chunks = sub // 2
    for r in range(CAP):
        stage[...] = got_ref[:, r].astype(f32).reshape(groups * sub, LANES)
        at = slice(r * groups, (r + 1) * groups)
        for c in range(chunks):
            cols = slice(c * LANES, (c + 1) * LANES)
            x_ref[at, cols] = stage[pl.ds(c, groups, stride=sub), :].astype(bf16)
            q_ref[at, cols] = stage[pl.ds(chunks + c, groups, stride=sub), :].astype(bf16)
    for copy in copies[:parts]:
        copy.wait()
    for copy in copies[parts : parts + 2]:
        copy.start()
    x = x_ref[...]
    a = mul(x, w_ref[0], NN)
    u = mul(x, w_ref[1], NN)
    dh = mul(q_ref[...], w_ref[2], NN)
    sig = jax.nn.sigmoid(a)
    silu = a * sig
    h = (silu * u).astype(bf16)
    da = (dh * u * (sig * (1.0 + a * (1.0 - sig)))).astype(bf16)
    du = (dh * silu).astype(bf16)
    h_ref[...] = h
    da_ref[...] = da
    du_ref[...] = du
    for copy in copies[parts + 2 : parts + 5]:
        copy.start()
    gate = jnp.sum(h.astype(f32) * dh, axis=1, keepdims=True)
    rows = mul(da, w_ref[0], NT) + mul(du, w_ref[1], NT)
    lines = stage_back.shape[0] // groups
    lane = lax.broadcasted_iota(jnp.int32, (groups, LANES), 1)
    gates = jnp.zeros((groups, LANES), f32)
    for r in range(CAP):
        at = slice(r * groups, (r + 1) * groups)
        for c in range(chunks):
            stage_back[pl.ds(r * chunks + c, groups, stride=lines), :] = rows[at, c * LANES : (c + 1) * LANES]
        gates = jnp.where(lane == r, gate[at], gates)
    stage_back[pl.ds(CAP * chunks, groups, stride=lines), :] = gates
    for spare in range(CAP * chunks + 1, lines):
        stage_back[pl.ds(spare, groups, stride=lines), :] = jnp.zeros((groups, LANES), f32)
    for k, cut in enumerate(cuts):
        packed = stage_back[k * portion * 8 : (k + 1) * portion * 8, :]
        back_ref[cut] = packed.reshape(portion, 8, LANES).astype(bf16)
        copies[parts + 5 + k].start()
    for copy in copies[parts:]:
        copy.wait()


def rows_step(place, got, pieces):
    groups, _, sub, _ = got.shape
    three, depth, hidden = pieces[0].shape
    width = depth * len(pieces)
    rows, chunks = groups * CAP, sub // 2
    lines = -(-(CAP * chunks + 1) // 2) * 2
    made = [(groups * lines // 8, 8, LANES)] + [(rows, width)] * 2 + [(rows, hidden)] * 3
    anywhere = pl.BlockSpec(memory_space=pl.ANY)
    return pl.pallas_call(
        rows_body,
        out_shape=[pltpu.HBM(s, bf16) for s in made],
        in_specs=[pl.BlockSpec(memory_space=pltpu.SMEM), pl.BlockSpec(memory_space=pltpu.VMEM)]
        + [anywhere] * len(pieces),
        out_specs=[anywhere] * len(made),
        scratch_shapes=[pltpu.VMEM(s, bf16) for s in [(three, width, hidden)] + made]
        + [pltpu.VMEM((groups * sub, LANES), f32), pltpu.VMEM((groups * lines, LANES), f32)]
        + [pltpu.SemaphoreType.DMA((len(pieces) + len(made) - 1 + PORTIONS,))],
        compiler_params=pltpu.CompilerParams(vmem_limit_bytes=44 * 2**20),
        cost_estimate=pl.CostEstimate(
            flops=10 * rows * width * hidden, bytes_accessed=8 * 2**20, transcendentals=0
        ),
    )(place, got, *pieces)


def grads_body(core_ref, x_ref, q_ref, da_ref, du_ref, h_ref, keep_ref, send_ref):
    halves, _, depth, _ = keep_ref.shape
    for out_ref, core in ((send_ref, 1 - core_ref[0]), (keep_ref, core_ref[0])):
        for half in range(halves):
            cols = pl.ds(pl.multiple_of((half * 2 + core) * depth, depth), depth)
            out_ref[half, 0] = mul(x_ref[:, cols], da_ref[...], TN).astype(bf16)
            out_ref[half, 1] = mul(x_ref[:, cols], du_ref[...], TN).astype(bf16)
            out_ref[half, 2] = mul(q_ref[:, cols], h_ref[...], TN).astype(bf16)


def weight_grads(core, x, q, da, du, h):
    rows, width = x.shape
    hidden = h.shape[1]
    vmem = pl.BlockSpec(memory_space=pltpu.VMEM)
    half = jax.ShapeDtypeStruct((2, 3, width // 4, hidden), bf16)
    return call(
        grads_body,
        (half, half),
        [],
        6 * rows * width * hidden,
        6 * 2**20,
        [pl.BlockSpec(memory_space=pltpu.SMEM)] + [vmem] * 5,
    )(core, x, q, da, du, h)


def pair_body(side_ref, keep_ref, got_ref, own_ref, send_ref):
    side = side_ref[0]
    send_ref[...] = (keep_ref[1 - side].astype(f32) + got_ref[1 - side].astype(f32)).astype(bf16)
    own_ref[...] = keep_ref[side].astype(f32) + got_ref[side].astype(f32)


def pair_sum(side, keep, got):
    vmem = pl.BlockSpec(memory_space=pltpu.VMEM)
    return pl.pallas_call(
        pair_body,
        out_shape=(
            jax.ShapeDtypeStruct(keep.shape[1:], f32),
            jax.ShapeDtypeStruct(keep.shape[1:], bf16),
        ),
        in_specs=[pl.BlockSpec(memory_space=pltpu.SMEM), vmem, vmem],
        out_specs=(vmem, vmem),
        compiler_params=pltpu.CompilerParams(vmem_limit_bytes=16 * 2**20),
        cost_estimate=pl.CostEstimate(flops=keep.size, bytes_accessed=5 * keep.size, transcendentals=0),
    )(side, keep, got)


def adam_body(own_ref, other_ref, one_ref, two_ref, out_ref):
    bands, blocks, sub, _ = out_ref.shape
    step = 16
    for p in range(0, bands, step):
        at = slice(p * sub, (p + step) * sub)
        grad = own_ref[at, :] + other_ref[at, :].astype(f32)
        first_new = BETA_ONE * one_ref[at, :] + (1.0 - BETA_ONE) * grad
        second_new = BETA_TWO * two_ref[at, :] + (1.0 - BETA_TWO) * grad * grad
        first_hat = first_new * (1.0 / (1.0 - BETA_ONE**STEP))
        second_hat = second_new * (1.0 / (1.0 - BETA_TWO**STEP))
        update = first_hat / (jnp.sqrt(second_hat) + ADAM_EPS)
        for b in range(blocks):
            tiles = update[:, b * LANES : (b + 1) * LANES].reshape(step, sub, LANES)
            out_ref[p : p + step, b] = tiles.astype(bf16)


def adam_update(own, other, moment_one, moment_two):
    rows, hidden = own.shape
    return call(
        adam_body,
        jax.ShapeDtypeStruct((rows // 8, hidden // LANES, 8, LANES), bf16),
        [],
        12 * own.size,
        14 * own.size,
    )(own, other, moment_one, moment_two)


def swap_body(partner_ref, in_ref, out_ref):
    def step(d, carry):
        out_ref[d] = in_ref[partner_ref[d]]
        return carry

    lax.fori_loop(0, in_ref.shape[0], step, 0, unroll=8)


def swap_slots(partner, spread):
    vmem = pl.BlockSpec(memory_space=pltpu.VMEM)
    return call(
        swap_body,
        jax.ShapeDtypeStruct(spread.shape, spread.dtype),
        [],
        0,
        4 * spread.size,
        [pl.BlockSpec(memory_space=pltpu.SMEM), vmem],
    )(partner, spread)


def combine_body(ids_ref, prob_ref, back_ref, tok_ref, gate_ref, stage, rows):
    groups, chunks = rows.shape[0] // CAP, rows.shape[1] // LANES
    lines = stage.shape[0] // groups
    hots, picks = routing(ids_ref[...], groups)
    stage[...] = back_ref[...].astype(f32).reshape(stage.shape)
    for r in range(CAP):
        for c in range(chunks):
            rows[r * groups : (r + 1) * groups, c * LANES : (c + 1) * LANES] = stage[
                pl.ds(r * chunks + c, groups, stride=lines), :
            ].astype(bf16)
    tok_ref[...] = mul(jnp.concatenate(picks, axis=0).astype(bf16), rows[...], TN).astype(bf16)
    gates = stage[pl.ds(CAP * chunks, groups, stride=lines), :]
    gate_at = sum(picks[r] * gates[:, r : r + 1] for r in range(CAP))
    for k in range(2):
        total = jnp.sum(jnp.where(hots[k], gate_at, 0.0), axis=0, keepdims=True)
        gate_ref[k : k + 1, :] = total / prob_ref[k : k + 1, :].astype(f32)


def combine(ids_t, prob_t, back, width, groups):
    tok_count = ids_t.shape[1]
    return call(
        combine_body,
        (
            jax.ShapeDtypeStruct((tok_count, width), bf16),
            jax.ShapeDtypeStruct((2, tok_count), f32),
        ),
        [
            pltpu.VMEM((back.size // LANES, LANES), f32),
            pltpu.VMEM((groups * CAP, width), bf16),
        ],
        2 * CAP * groups * tok_count * width,
        4 * 2**20,
    )(ids_t, prob_t, back)


def on_device(
    tokens,
    cotangent,
    route_ids,
    gate_prob,
    swap_partner,
    expert_weights,
    first_moment,
    second_moment,
):
    groups = lax.axis_size("expert")
    hidden = expert_weights.shape[3]
    flat = (expert_weights.size // hidden, hidden)
    ids_t, prob_t = route_ids.T, gate_prob.T
    replica = lax.axis_index("dp")
    core, side = (replica % 2).reshape(1), (replica // 2).reshape(1)
    tiles, pairs = (-1, 8, LANES), (groups, -1, 2, LANES)

    sent = dispatch(ids_t, prob_t, tokens, cotangent, groups)
    mine, sent = lax.optimization_barrier((expert_weights[0], sent))
    got = exchange(sent)
    far = lax.ppermute(mine, "dp", ACROSS)
    pieces = (mine, far, lax.ppermute(mine, "dp", BESIDE), lax.ppermute(far, "dp", BESIDE))
    near = side * 2
    place = jnp.concatenate([near + core, 2 - near + core, near + 1 - core, 3 - near - core])
    returned, *operands = rows_step(place, got, pieces)
    keep, sent = weight_grads(core, *operands)
    own, sent = pair_sum(side, keep, lax.ppermute(sent, "dp", BESIDE))
    back = exchange(returned.reshape(pairs))
    other = lax.ppermute(sent, "dp", ACROSS)
    staged = adam_update(
        own.reshape(flat), other.reshape(flat), first_moment.reshape(flat), second_moment.reshape(flat)
    )
    back, staged = lax.optimization_barrier((back, staged))
    spread = exchange(staged.reshape(pairs))
    routed = exchange(swap_slots(swap_partner, spread))
    token_grad, gate_grad = combine(ids_t, prob_t, back.reshape(tiles), tokens.shape[1], groups)
    update = routed.reshape(staged.shape).transpose(0, 2, 1, 3)
    return (token_grad, gate_grad.T.astype(bf16), update.reshape(expert_weights.shape))


def solution(mesh):
    placed = (
        P(("expert", "dp"), None),
        P(("expert", "dp"), None),
        P(("expert", "dp"), None),
        P(("expert", "dp"), None),
        P(),
        P("expert", None, "dp", None),
        P("expert", None, "dp", None),
        P("expert", None, "dp", None),
    )
    return jax.shard_map(
        on_device,
        mesh=mesh,
        in_specs=placed,
        out_specs=(
            P(("expert", "dp"), None),
            P(("expert", "dp"), None),
            P("expert", None, "dp", None),
        ),
        check_vma=False,
    )
```
